512 devices in a mesh: section: 16 (over x_lo, y, core), expert: 32 (over x_hi, z).
Axes of the slice: x: 4 (x_hi: 2, x_lo: 2; x = x_hi * 2 + x_lo), y: 4, z: 16, core: 2. Of those that a mesh axis runs over, the one named last changes fastest.
Arguments:
- tokens: bfloat16 [4608, 3584], P('expert', 'section'), may hold values from -6 to 6
- norm_gain: bfloat16 [1, 3584], P(None, 'section'), may hold values from 0.5 to 1.5
- expert_ids: int32 [4608, 2], P('expert'), may hold values from 0 to 31, all different within a row; in each aligned block of 144 rows (0 to 143, 144 to 287, ...) at most 18 rows name the same one
- gate_weight: float32 [4608, 2], P('expert'), may hold values from 0.2 to 1
- w_gate: bfloat16 [32, 3584, 2048], P('expert', None, 'section'), may hold values from -0.09375 to 0.09375
- w_up: bfloat16 [32, 3584, 2048], P('expert', None, 'section'), may hold values from -0.09375 to 0.09375
- w_down: bfloat16 [32, 2048, 3584], P('expert', 'section'), may hold values from -0.125 to 0.125
Outputs:
- mixed_out: bfloat16 [4608, 3584], P('expert', 'section')
The draws below stay inside these ranges and needn't reach their ends.
Inputs may be any that keep to these rules, and one draw needn't show every extreme that they name: `expert_ids`: each token names 2 different experts; among the 144 tokens of one index of the expert axis no expert is named more than 18 times, a bound that some block reaches.
All inputs are finite; a program needn't handle non-finite values.
Results may differ from the reference program's by a relative error of at most 0.023.
Values may be sent and summed in bfloat16 or wider, within the bound.
A program may use at most 128 MiB of HBM per device.

```python
import math
import jax
import jax.numpy as jnp
import numpy as np
from jax import lax

D = 3584
FE = 2048
TOPW = 2
TOK_DEV = 144
HID = 128
EXPERTS = 32
CAP = 18
TOKENS = 4608
N_SECTION = 16
N_EXPERT = 32


def steps_of(own_key, shape, split, low, largest):
    def one(dim, shards_of):
        draws = jax.random.uniform(jax.random.fold_in(jax.random.fold_in(own_key, 6), dim), (shards_of,), jnp.float32, low / len(split), largest / len(split))
        return jnp.repeat(jnp.exp(draws), shape[dim] // shards_of).reshape((-1,) + (1,) * (len(shape) - dim - 1))

    factor_of = one(*split[0])
    for cut in split[1:]:
        factor_of = factor_of * one(*cut)
    return factor_of


def assign_block(rng, own, number, rows, count, top, reach, lean):
    ranking = jax.random.permutation(rng, count)
    packed, common = shares(count, rows * top, reach, lean, True), shares(count, rows * top, reach, lean, False)
    places = jnp.arange(count)

    def named(sizes, offset_by):
        used = int((sizes > 0).sum())
        fixed = max(1, used // 4)
        shifted = fixed + (places - fixed + offset_by * (used - fixed)) % max(1, count - fixed)
        return jnp.zeros((count,), jnp.int32).at[ranking[jnp.where(places < fixed, places, shifted)]].set(jnp.asarray(sizes, jnp.int32))

    sizes = jnp.where(number % 4 == 0, named(packed, number // 4), named(common, number - number // 4 - 1))
    mixed = jax.random.permutation(jax.random.fold_in(own, 3), count)
    source_of, receiver = mixed[0:count // 2 * 2:2], mixed[1:count // 2 * 2:2]
    slack = jnp.minimum(sizes[source_of] - 1, reach - sizes[receiver]) // 2
    slack = jnp.where((source_of == ranking[0]) | (receiver == ranking[0]) | (sizes[receiver] == 0), 0, jnp.maximum(slack, 0))
    shifted = jax.random.randint(jax.random.fold_in(own, 4), (count // 2,), 0, 1 << 20) % (slack + 1)
    sizes = sizes.at[source_of].add(-shifted).at[receiver].add(shifted)
    items = jnp.searchsorted(jnp.cumsum(sizes), jnp.arange(rows * top), side="right").astype(jnp.int32)
    listing = items.reshape(top, rows).T
    listing = listing[jax.random.permutation(jax.random.fold_in(own, 1), rows)]
    offset_by = jax.random.randint(jax.random.fold_in(own, 2), (rows, 1), 0, top)
    return jnp.take_along_axis(listing, (jnp.arange(top)[None, :] + offset_by) % top, axis=1)


def shares(count, total, bound, lean, full):
    weights = [(1 << 20) // math.isqrt(grade ** lean) + 1 for grade in range(1, count + 1)]
    largest = bound if full else min(bound, max(-(-total // count), total * weights[0] // sum(weights)))
    least = 1 if total - largest >= count - 1 else 0
    holding, spare = [largest] + [least] * (count - 1), total - largest - least * (count - 1)
    while spare > 0:
        movable = [i for i in range(1, count) if holding[i] < largest] or [i for i in range(1, count) if holding[i] < bound]
        mass, left = sum([weights[i] for i in movable]), spare
        for i in movable:
            extra = min(bound - holding[i], max(1, left * weights[i] // mass), spare)
            holding[i] = holding[i] + extra
            spare = spare - extra
    return np.array(holding)


def gaussian(rng, dims, width, reach, pieces=(), held_as=jnp.bfloat16):
    level = steps_of(rng, dims, pieces, -0.22, 0.18) if pieces else 1.0
    drawn = jax.random.normal(rng, dims, jnp.float32) * width * level
    return jnp.minimum(jnp.maximum(drawn, -reach), reach).astype(held_as)


def setup_inputs(seed: int = 0) -> dict:
    keys = jax.random.split(jax.random.key(seed), 8)
    tokens = gaussian(keys[0], (TOKENS, D), 1.0, 6.0, ((0, 32), (1, 16)))
    norm_gain = jnp.clip(0.5 + 1.0 * jax.random.uniform(keys[1], (1, D), jnp.float32) ** steps_of(keys[1], (1, D), ((1, 16),), -0.2, 0.2), 0.5, 1.5).astype(jnp.bfloat16)
    expert_ids_keys = jax.random.split(jax.random.fold_in(keys[2], 1), TOKENS // TOK_DEV)
    expert_ids_turns = jax.random.permutation(jax.random.fold_in(keys[2], 3), TOKENS // TOK_DEV)
    expert_ids = jax.vmap(lambda own, number: assign_block(jax.random.fold_in(keys[2], 2), own, number, TOK_DEV, EXPERTS, TOPW, CAP, 2))(expert_ids_keys, expert_ids_turns).reshape((TOKENS, TOPW))
    gate_weight = jnp.clip(0.2 + 0.8 * jax.random.uniform(keys[3], (TOKENS, TOPW), jnp.float32) ** steps_of(keys[3], (TOKENS, TOPW), ((0, 32),), -0.2, 0.2), 0.2, 1.0)
    w_gate = gaussian(keys[4], (EXPERTS, D, FE), D ** -0.5, 0.09375, ((0, 32), (2, 16)))
    w_up = gaussian(keys[5], (EXPERTS, D, FE), D ** -0.5, 0.09375, ((0, 32), (2, 16)))
    w_down = gaussian(keys[6], (EXPERTS, FE, D), FE ** -0.5, 0.125, ((0, 32), (1, 16)))
    return {"tokens": tokens, "norm_gain": norm_gain, "expert_ids": expert_ids, "gate_weight": gate_weight, "w_gate": w_gate, "w_up": w_up, "w_down": w_down}


epsilon = 1e-06

def reference(tokens, norm_gain, expert_ids, gate_weight, w_gate, w_up, w_down):
    floats = tokens.astype(jnp.float32)
    mean_square = lax.optimization_barrier(jnp.mean(floats * floats, axis=1, keepdims=True))
    normed = (floats * lax.rsqrt(mean_square + epsilon) * norm_gain.astype(jnp.float32)).astype(jnp.bfloat16)
    token_count = tokens.shape[0]
    flat_ids = expert_ids.reshape(-1).astype(jnp.int32)
    onehot = (flat_ids[:, None] == jnp.arange(EXPERTS, dtype=jnp.int32)[None, :]).astype(jnp.int32)
    onehot = onehot.reshape(N_EXPERT, TOK_DEV * TOPW, EXPERTS)
    before = jnp.cumsum(onehot, axis=1) - onehot
    slot = lax.optimization_barrier(jnp.sum(before * onehot, axis=2)).reshape(-1).astype(jnp.int32)
    source = (jnp.arange(token_count * TOPW, dtype=jnp.int32) // (TOK_DEV * TOPW)).astype(jnp.int32)
    position = (flat_ids * (N_EXPERT * CAP) + source * CAP + slot).astype(jnp.int32)
    routed = jnp.repeat(normed.astype(jnp.float32), TOPW, axis=0)
    buffers = jnp.zeros((EXPERTS * N_EXPERT * CAP, D), jnp.float32).at[position].set(routed)
    buffers = buffers.reshape(EXPERTS, N_EXPERT * CAP, D)

    def expert_block(inputs):
        rows_in, gate_matrix, up_matrix, down_matrix = inputs
        gate_pre = jnp.dot(rows_in, gate_matrix.astype(jnp.float32), precision=lax.Precision.HIGHEST)
        up_pre = jnp.dot(rows_in, up_matrix.astype(jnp.float32), precision=lax.Precision.HIGHEST)
        hidden_low = lax.optimization_barrier((jax.nn.silu(gate_pre) * up_pre).astype(jnp.bfloat16))
        hidden = hidden_low.astype(jnp.float32).reshape(-1, N_SECTION, HID)
        down_blocks = down_matrix.astype(jnp.float32).reshape(N_SECTION, HID, D)
        partial_value = jnp.einsum('mjh,jhd->jmd', hidden, down_blocks, precision=lax.Precision.HIGHEST)
        rounded = lax.optimization_barrier(partial_value.astype(jnp.bfloat16)).astype(jnp.float32)
        return lax.optimization_barrier(jnp.sum(rounded, axis=0))
    outputs = lax.map(expert_block, (buffers, w_gate, w_up, w_down))
    picked = outputs.reshape(-1, D)[position].reshape(token_count, TOPW, D)
    return lax.optimization_barrier(jnp.sum(gate_weight[:, :, None] * picked, axis=1)).astype(jnp.bfloat16)
```

```python
import jax
import jax.numpy as jnp
from jax import lax
from jax.sharding import PartitionSpec as P

epsilon = 1e-06


def slot_table(expert_ids, experts, capacity):
    token_count, routes = expert_ids.shape
    flat_ids = expert_ids.reshape(-1)
    onehot = (flat_ids[:, None] == jnp.arange(experts, dtype=jnp.int32)[None, :]).astype(jnp.int32)
    before = jnp.cumsum(onehot, axis=0) - onehot
    slot = jnp.sum(before * onehot, axis=1)
    return (flat_ids * capacity + slot).reshape(token_count, routes)


def on_device(tokens, norm_gain, expert_ids, gate_weight, w_gate, w_up, w_down):
    experts = lax.axis_size("expert")
    token_count, routes = expert_ids.shape
    capacity = 2 * token_count * routes // experts
    position = slot_table(expert_ids, experts, capacity)
    places = jnp.arange(experts * capacity, dtype=jnp.int32)
    dispatch_map = jnp.sum(
        (places[:, None, None] == position[None, :, :]).astype(jnp.int32), axis=2
    ).astype(jnp.bfloat16)
    gate_matrix = w_gate[0]
    up_matrix = w_up[0]
    buffer = jnp.dot(dispatch_map, tokens, preferred_element_type=jnp.float32).astype(jnp.bfloat16)
    buffer = buffer.reshape(experts, capacity, tokens.shape[1])
    own_part = lax.all_to_all(buffer, "expert", split_axis=0, concat_axis=0, tiled=True).reshape(
        experts * capacity, tokens.shape[1]
    )
    with_gain = jnp.concatenate(
        [own_part, jnp.broadcast_to(norm_gain, (16, norm_gain.shape[1]))], axis=0
    )
    gathered = lax.all_gather(with_gain, "section", axis=1, tiled=True)
    floats = gathered[: experts * capacity].astype(jnp.float32)
    gain_full = gathered[experts * capacity : experts * capacity + 1]
    mean_square = jnp.mean(floats * floats, axis=1, keepdims=True)
    arrived = (floats * lax.rsqrt(mean_square + epsilon) * gain_full.astype(jnp.float32)).astype(
        jnp.bfloat16
    )
    gate_pre = jnp.dot(arrived, gate_matrix, preferred_element_type=jnp.float32)
    up_pre = jnp.dot(arrived, up_matrix, preferred_element_type=jnp.float32)
    hidden = (jax.nn.silu(gate_pre) * up_pre).astype(jnp.bfloat16)
    partial_value = jnp.dot(hidden, w_down[0], preferred_element_type=jnp.float32)
    rounded = lax.optimization_barrier(partial_value.astype(jnp.bfloat16))
    summed = lax.psum_scatter(
        rounded.astype(jnp.float32).astype(jnp.bfloat16), "section", scatter_dimension=1, tiled=True
    ).astype(jnp.float32)
    returned_rows = lax.all_to_all(
        summed.reshape(experts, capacity, summed.shape[1]).astype(jnp.bfloat16),
        "expert",
        split_axis=0,
        concat_axis=0,
        tiled=True,
    ).astype(jnp.float32)
    returned_rows = returned_rows.reshape(experts * capacity, summed.shape[1])
    picked = returned_rows[position]
    mixed_out = jnp.sum(gate_weight[:, :, None] * picked, axis=1).astype(jnp.bfloat16)
    return mixed_out


def solution(mesh):
    placed = (
        P("expert", "section"),
        P(None, "section"),
        P("expert", None),
        P("expert", None),
        P("expert", None, "section"),
        P("expert", None, "section"),
        P("expert", "section", None),
    )
    return jax.shard_map(
        on_device, mesh=mesh, in_specs=placed, out_specs=P("expert", "section"), check_vma=False
    )
```

```python
import jax
import jax.numpy as jnp
from jax import lax
from jax.experimental import pallas as pl
from jax.experimental.pallas import tpu as pltpu
from jax.sharding import PartitionSpec as P

epsilon = 1e-06
D = 3584
FEAT = 224
LANES = 256
TOK = 144
SLOTS = 16
GROUPS = 4
PER = 8
MAIN = PER * SLOTS
ROWS = MAIN + 2 * PER
F32 = jnp.float32
BF16 = jnp.bfloat16
I32 = jnp.int32
MESH = pl.DeviceIdType.MESH


def iota(shape, dim):
    return lax.broadcasted_iota(I32, shape, dim)


def one_hot(mask):
    return jnp.where(mask, 1.0, 0.0).astype(BF16)


def dot(a, b):
    return jnp.dot(a, b, preferred_element_type=F32)


def peer_expert(place, xh, z, sign):
    step = place // 2
    half = (step + 1) // 2
    offset = half * (2 * (step % 2) - 1)
    return ((xh + place % 2) % 2) * 16 + (z + sign * offset + 16) % 16


def piece_of(slot):
    return slot - 7 * (slot >= 7).astype(I32)


def unfold(packed):
    rows = packed.shape[0]
    lane = iota((128, LANES), 1)
    spread = one_hot((iota((128, LANES), 0) - 96 == lane % 32) & (lane < FEAT))
    copies = dot(packed[:, 128:256], spread)
    slot = iota((rows, LANES), 0) % 16
    keep = (iota((rows, LANES), 1) // 32 == piece_of(slot)) & (slot < 14)
    return jnp.where(keep, copies, 0.0).astype(BF16)


def fold(spread):
    rows, width = spread.shape
    slot = iota((rows, width), 0) % 16
    keep = (iota((rows, width), 1) // 32 == piece_of(slot)) & (slot < 14)
    own = jnp.where(keep, spread, 0.0).astype(BF16)
    lane = iota((width, LANES), 1)
    gather = one_hot((lane >= FEAT) & (iota((width, LANES), 0) % 32 == lane - FEAT))
    return dot(own, gather)


def kernel(
    tokens, ids, ids_t, gate_weight, gain, w_gate, w_up, w_down, out,
    pack, arrived, blocks, wide, down, down_raw, hidden, core_out, core_in, sums, y_in, x_out, x_in,
    back, returned, picks, total0, total1,
    w_sem, z_send, z_recv, g_send, g_x, g_y, g_core, p_send, p_recv, r_send, r_recv, x_send, x_recv,
    b_send, b_recv,
):
    section, expert = lax.axis_index("section"), lax.axis_index("expert")
    xl, y, core = section // 8, (section // 2) % 4, section % 2
    xh, z = expert // 16, expert % 16
    up, dn, far = (y + 1) % 4, (y + 3) % 4, (y + 2) % 4
    ox = 1 - xl

    def sec(a, b, c):
        return ((a * 4 + b) * 2 + c, expert)

    to_x, to_up, to_dn, to_core = sec(ox, y, core), sec(xl, up, core), sec(xl, dn, core), sec(xl, y, 1 - core)

    barrier = pltpu.get_barrier_semaphore()
    for peer in (to_core, to_x, to_up, to_dn):
        pl.semaphore_signal(barrier, inc=1, device_id=peer, device_id_type=MESH)

    @pl.loop(1, 32)
    def _(place):
        pl.semaphore_signal(
            barrier, inc=1, device_id=(section, peer_expert(place, xh, z, 1)), device_id_type=MESH
        )

    loads = []
    for half, ref in enumerate((w_gate, w_up)):
        for c in range(2):
            loads.append(
                pltpu.make_async_copy(
                    ref.at[:, c],
                    wide.at[pl.ds(8 * c, 8), pl.ds(0, FEAT), pl.ds(128 * half, 128)],
                    w_sem.at[2 * half + c],
                )
            )
    loads.append(pltpu.make_async_copy(w_down, down_raw, w_sem.at[4]))
    for load in loads:
        load.start()

    def send(src, dst, send_sem, recv_sem, peer):
        pltpu.make_async_remote_copy(
            src_ref=src, dst_ref=dst, send_sem=send_sem, recv_sem=recv_sem, device_id=peer, device_id_type=MESH
        ).start()

    def await_bytes(ref, sem):
        pltpu.make_async_copy(ref, ref, sem).wait()

    keys_t = []
    named = [(iota((32, TOK), 0) == ids_t[k : k + 1, :]) for k in range(2)]
    before = dot(
        one_hot(named[0] | named[1]), one_hot(iota((TOK, TOK), 0) < iota((TOK, TOK), 1))
    )
    for k in range(2):
        number = jnp.sum(jnp.where(named[k], before, 0.0), axis=0, keepdims=True)
        keys_t.append(ids_t[k : k + 1, :] * 32 + number.astype(I32))
    row = iota((512, 1), 0)
    base, slot = peer_expert(row // 16, xh, z, -1) * 32, row % 16
    main_key = base + slot
    rest_key = jnp.where(slot < 14, base + 16 + (slot >= 7).astype(I32), -1)
    to_main = one_hot((keys_t[0] == main_key) | (keys_t[1] == main_key))
    to_rest = one_hot((keys_t[0] == rest_key) | (keys_t[1] == rest_key))
    widen = one_hot(iota((FEAT, LANES), 0) == iota((FEAT, LANES), 1))
    padded = dot(tokens[...], widen).astype(BF16)
    packed = dot(to_main, padded) + fold(dot(to_rest, padded))
    pack[...] = packed.astype(BF16).reshape(32, 16, LANES)
    arrived[0] = pack[0]

    pl.semaphore_wait(barrier, 35)

    @pl.loop(1, 32)
    def _(place):
        send(
            pack.at[place], arrived.at[place], z_send, z_recv.at[place // PER],
            (section, peer_expert(place, xh, z, -1)),
        )

    named = [(iota((TOK, 128), 1) == ids[:, k : k + 1]) for k in range(2)]
    before = dot(
        one_hot(iota((TOK, TOK), 1) < iota((TOK, TOK), 0)), one_hot(named[0] | named[1])
    )
    for k in range(2):
        number = jnp.sum(jnp.where(named[k], before, 0.0), axis=1, keepdims=True)
        key = ids[:, k : k + 1] * 32 + number.astype(I32)
        for q in range(GROUPS):
            column = iota((1, MAIN), 1) + q * MAIN
            base, slot = peer_expert(column // 16, xh, z, -1) * 32, column % 16
            rest_key = jnp.where(slot < 14, base + 16 + (slot >= 7).astype(I32), -1)
            picks[q, 0, pl.ds(k * TOK, TOK), :] = one_hot(key == base + slot)
            picks[q, 1, pl.ds(k * TOK, TOK), :] = one_hot(key == rest_key)
    total0[...] = jnp.zeros_like(total0)
    total1[...] = jnp.zeros_like(total1)

    gain_row = dot(jnp.broadcast_to(gain[...], (16, FEAT)), widen)[0:1, :]
    wide[:, FEAT:LANES, :] = jnp.zeros((16, LANES - FEAT, LANES), BF16)
    for load in loads:
        load.wait()
    for s in range(16):
        first = (s * FEAT) // 128 * 128
        shift = s * FEAT - first
        window = down_raw[:, first : first + (384 if shift else 256)] if first + 384 <= D or not shift else down_raw[:, first:D]
        piece = window.astype(F32)[:, shift : shift + FEAT]
        down[(s % 2) * 8 + s // 2, :, 0:FEAT] = piece.astype(BF16)
        down[(s % 2) * 8 + s // 2, :, FEAT:LANES] = jnp.zeros((128, LANES - FEAT), BF16)

    def chip(a, b):
        return a * 4 + b

    def block(q, a, b, c):
        return blocks.at[q, c * 8 + chip(a, b)]

    def share(q, a, b, peer, recv_sem):
        ref = block(q, a, b, core)
        send(ref, ref, g_send.at[q], recv_sem, peer)

    def to_peer(q, a, b):
        share(q, a, b, to_core, g_core.at[q])

    def unpack(q):
        @pl.when(q == 0)
        def _():
            await_bytes(arrived.at[pl.ds(1, PER - 1)], z_recv.at[0])

        @pl.when(q > 0)
        def _():
            await_bytes(arrived.at[pl.ds(q * PER, PER)], z_recv.at[q])

        got = arrived[pl.ds(q * PER, PER)].reshape(MAIN, LANES)
        lane = iota((ROWS, LANES), 1)
        row, col = iota((2 * PER, MAIN), 0), iota((2 * PER, MAIN), 1)
        slot = col % 16
        gather = one_hot((col // 16 == row // 2) & (slot < 14) & ((slot >= 7).astype(I32) == row % 2))
        rest = dot(gather, unfold(got))
        x = jnp.where(lane < FEAT, jnp.concatenate([got.astype(F32), rest], axis=0), 0.0)
        square = jnp.sum(x * x, axis=1, keepdims=True)
        high = square.astype(BF16).astype(F32)
        mid = (square - high).astype(BF16).astype(F32)
        low = square - high - mid
        x = x * gain_row
        x = jnp.where(lane == FEAT, high, x)
        x = jnp.where(lane == FEAT + 1, mid, x)
        x = jnp.where(lane == FEAT + 2, low, x)
        blocks[q, core * 8 + chip(xl, y)] = x.astype(BF16)
        share(q, xl, y, to_x, g_x.at[q])
        share(q, xl, y, to_up, g_y.at[q, 0])
        share(q, xl, y, to_dn, g_y.at[q, 2])
        to_peer(q, xl, y)

    def gather_x(q):
        await_bytes(block(q, ox, y, core), g_x.at[q])
        share(q, ox, y, to_up, g_y.at[q, 3])
        share(q, ox, y, to_dn, g_y.at[q, 1])
        to_peer(q, ox, y)

    def gather_y(q):
        await_bytes(block(q, xl, dn, core), g_y.at[q, 0])
        share(q, xl, dn, to_up, g_y.at[q, 4])
        await_bytes(block(q, ox, up, core), g_y.at[q, 1])
        share(q, ox, up, to_dn, g_y.at[q, 5])
        to_peer(q, xl, dn)
        to_peer(q, ox, up)
        await_bytes(block(q, xl, up, core), g_y.at[q, 2])
        to_peer(q, xl, up)
        await_bytes(block(q, ox, dn, core), g_y.at[q, 3])
        to_peer(q, ox, dn)

    def gather_far(q):
        await_bytes(block(q, xl, far, core), g_y.at[q, 4])
        to_peer(q, xl, far)
        await_bytes(block(q, ox, far, core), g_y.at[q, 5])
        to_peer(q, ox, far)

    def compute(q):
        await_bytes(blocks.at[q, pl.ds((1 - core) * 8, 8)], g_core.at[q])
        product = jnp.zeros((ROWS, LANES), F32)
        squares = jnp.zeros((ROWS, 128), F32)
        for k in range(16):
            x = blocks[q, k]
            product = product + dot(x, wide[k])
            squares = squares + x[:, 128:256].astype(F32)
        lane = iota((ROWS, 128), 1)
        kept = (lane >= FEAT - 128) & (lane < FEAT - 128 + 3)
        square = jnp.sum(jnp.where(kept, squares, 0.0), axis=1, keepdims=True)
        scale = lax.rsqrt(square * (1.0 / D) + epsilon)
        gate, upward = product[:, 0:128] * scale, product[:, 128:256] * scale
        hidden[...] = (gate / (1.0 + jnp.exp(-gate)) * upward).astype(BF16)
        for k in range(8):
            core_out[q, k] = dot(hidden[...], down[(1 - core) * 8 + k]).astype(BF16)
        send(core_out.at[q], core_in.at[q], p_send.at[q], p_recv.at[q], to_core)

    def add_core(q):
        await_bytes(core_in.at[q], p_recv.at[q])
        for k in range(8):
            own = dot(hidden[...], down[core * 8 + k])
            sums[q, k] = (own + core_in[q, k].astype(F32)).astype(BF16)
        send(sums.at[q, chip(xl, far)], y_in.at[q, 0], r_send.at[q], r_recv.at[q, 0], to_up)
        send(sums.at[q, chip(ox, far)], y_in.at[q, 1], r_send.at[q], r_recv.at[q, 1], to_dn)
        send(sums.at[q, chip(ox, up)], y_in.at[q, 2], r_send.at[q], r_recv.at[q, 2], to_up)
        send(sums.at[q, chip(xl, dn)], y_in.at[q, 3], r_send.at[q], r_recv.at[q, 3], to_dn)

    def add_far(q):
        for j, where_to, peer in ((0, chip(xl, up), to_up), (1, chip(ox, dn), to_dn)):
            await_bytes(y_in.at[q, j], r_recv.at[q, j])
            sums[q, where_to] = (sums[q, where_to].astype(F32) + y_in[q, j].astype(F32)).astype(BF16)
            send(sums.at[q, where_to], y_in.at[q, 4 + j], r_send.at[q], r_recv.at[q, 4 + j], peer)

    def add_y(q):
        for j in (2, 5):
            await_bytes(y_in.at[q, j], r_recv.at[q, j])
        x_out[q] = (
            sums[q, chip(ox, y)].astype(F32) + y_in[q, 2].astype(F32) + y_in[q, 5].astype(F32)
        ).astype(BF16)
        send(x_out.at[q], x_in.at[q], x_send.at[q], x_recv.at[q], to_x)
        for j in (3, 4):
            await_bytes(y_in.at[q, j], r_recv.at[q, j])

    def add_x(q):
        own = sums[q, chip(xl, y)].astype(F32) + y_in[q, 3].astype(F32) + y_in[q, 4].astype(F32)
        await_bytes(x_in.at[q], x_recv.at[q])
        total = own + x_in[q].astype(F32)
        row, col = iota((MAIN, 2 * PER), 0), iota((MAIN, 2 * PER), 1)
        slot = row % 16
        spread = one_hot((row // 16 == col // 2) & (slot < 14) & ((slot >= 7).astype(I32) == col % 2))
        packed = total[0:MAIN] + fold(dot(spread, total[MAIN:ROWS].astype(BF16)))
        back[pl.ds(q * PER, PER)] = packed.astype(BF16).reshape(PER, 16, LANES)

        @pl.when(q == 0)
        def _():
            returned[0] = back[0]

        @pl.loop(jnp.where(q == 0, 1, 0), PER)
        def _(k):
            place = q * PER + k
            send(
                back.at[place], returned.at[place], b_send, b_recv.at[q],
                (section, peer_expert(place, xh, z, 1)),
            )

    def mix(q):
        @pl.when(q == 0)
        def _():
            await_bytes(returned.at[pl.ds(1, PER - 1)], b_recv.at[0])

        @pl.when(q > 0)
        def _():
            await_bytes(returned.at[pl.ds(q * PER, PER)], b_recv.at[q])

        got = returned[pl.ds(q * PER, PER)].reshape(MAIN, LANES)
        picked = dot(picks[q, 0], got) + dot(picks[q, 1], unfold(got))
        total0[...] += picked[0:TOK]
        total1[...] += picked[TOK : 2 * TOK]

    stages = (unpack, gather_x, gather_y, gather_far, compute, add_core, add_far, add_y, add_x, mix)
    skew = (0, 1, 2, 3, 3, 4, 5, 6, 7, 8)

    @pl.loop(0, GROUPS + skew[-1])
    def _(step):
        for stage, late in sorted(zip(stages, skew), key=lambda pair: -pair[1]):
            q = step - late

            @pl.when((q >= 0) & (q < GROUPS))
            def _():
                stage(q)

    mixed = gate_weight[:, 0:1] * total0[...] + gate_weight[:, 1:2] * total1[...]
    out[...] = mixed[:, 0:FEAT].astype(BF16)

    await_bytes(pack.at[pl.ds(1, 31)], z_send)
    await_bytes(back.at[pl.ds(1, 31)], b_send)

    @pl.loop(0, GROUPS)
    def _(q):
        await_bytes(blocks.at[q, pl.ds(0, 15)], g_send.at[q])
        await_bytes(core_out.at[q], p_send.at[q])
        await_bytes(y_in.at[q], r_send.at[q])
        await_bytes(x_out.at[q], x_send.at[q])


def on_device(tokens, norm_gain, expert_ids, gate_weight, w_gate, w_up, w_down):
    vmem = pl.BlockSpec(memory_space=pltpu.VMEM)
    anywhere = pl.BlockSpec(memory_space=pl.ANY)
    dma = pltpu.SemaphoreType.DMA
    block = (ROWS, LANES)
    return pl.pallas_call(
        kernel,
        out_shape=jax.ShapeDtypeStruct((TOK, FEAT), BF16),
        in_specs=[vmem] * 5 + [anywhere] * 3,
        out_specs=vmem,
        scratch_shapes=[
            pltpu.VMEM((32, 16, LANES), BF16),
            pltpu.VMEM((32, 16, LANES), BF16),
            pltpu.VMEM((GROUPS, 16) + block, BF16),
            pltpu.VMEM((16, LANES, LANES), BF16),
            pltpu.VMEM((16, 128, LANES), BF16),
            pltpu.VMEM((128, D), BF16),
            pltpu.VMEM((ROWS, 128), BF16),
            pltpu.VMEM((GROUPS, 8) + block, BF16),
            pltpu.VMEM((GROUPS, 8) + block, BF16),
            pltpu.VMEM((GROUPS, 8) + block, BF16),
            pltpu.VMEM((GROUPS, 6) + block, BF16),
            pltpu.VMEM((GROUPS,) + block, BF16),
            pltpu.VMEM((GROUPS,) + block, BF16),
            pltpu.VMEM((32, 16, LANES), BF16),
            pltpu.VMEM((32, 16, LANES), BF16),
            pltpu.VMEM((GROUPS, 2, 2 * TOK, MAIN), BF16),
            pltpu.VMEM((TOK, LANES), F32),
            pltpu.VMEM((TOK, LANES), F32),
            dma((5,)), dma, dma((GROUPS,)),
            dma((GROUPS,)), dma((GROUPS,)), dma((GROUPS, 6)), dma((GROUPS,)),
            dma((GROUPS,)), dma((GROUPS,)),
            dma((GROUPS,)), dma((GROUPS, 6)),
            dma((GROUPS,)), dma((GROUPS,)),
            dma, dma((GROUPS,)),
        ],
        compiler_params=pltpu.CompilerParams(
            collective_id=0, has_side_effects=True, vmem_limit_bytes=48 * 1024 * 1024
        ),
        cost_estimate=pl.CostEstimate(flops=2_000_000_000, bytes_accessed=3_000_000, transcendentals=73728),
    )(
        tokens, expert_ids, expert_ids.T, gate_weight, norm_gain,
        w_gate.reshape(8, 2, FEAT, 128), w_up.reshape(8, 2, FEAT, 128), w_down[0],
    )


def solution(mesh):
    placed = (
        P("expert", "section"),
        P(None, "section"),
        P("expert", None),
        P("expert", None),
        P("expert", None, "section"),
        P("expert", None, "section"),
        P("expert", "section", None),
    )
    return jax.shard_map(
        on_device, mesh=mesh, in_specs=placed, out_specs=P("expert", "section"), check_vma=False
    )
```

```python
import jax
import jax.numpy as jnp
from jax import lax
from jax.experimental import pallas as pl
from jax.experimental.pallas import tpu as pltpu
from jax.sharding import PartitionSpec as P

epsilon = 1e-06
D = 3584
FEAT = 224
LANES = 256
TOK = 144
SLOTS = 16
GROUPS = 4
PER = 8
MAIN = PER * SLOTS
ROWS = MAIN + 2 * PER
F32 = jnp.float32
BF16 = jnp.bfloat16
I32 = jnp.int32
MESH = pl.DeviceIdType.MESH
SEND_ORDER = (0, 3, 2, 1)
GATHER_X_FIRST = (True, True, False, True)
SCATTER_X_FIRST = (False, False, False, True)
ORDER = (
    ("U", 0), ("W", 0), ("X", 0), ("Y0", 0), ("Y2", 0), ("U", 3), ("K", 0), ("Y3", 0), ("Y1", 0), ("F0", 0),
    ("X", 3), ("Y2", 3), ("U", 2), ("Y0", 3), ("F1", 0), ("U", 1), ("C", 0), ("Y1", 3), ("Y3", 3), ("y0", 2),
    ("x0", 2), ("X", 1), ("F0", 3), ("Y2", 1), ("R1", 0), ("Y0", 1), ("x1", 2), ("F1", 3), ("f0", 2), ("C", 3),
    ("Y1", 1), ("Y3", 1), ("x2", 2), ("R2a", 0), ("x3", 2), ("R2b", 0), ("R1", 3), ("C", 2), ("F0", 1), ("F1", 1),
    ("r2", 3), ("R3", 0), ("R1", 2), ("C", 1), ("r3", 3), ("R2a", 2), ("R2b", 2), ("R1", 1), ("R4", 0), ("R4", 3),
    ("Z", 0), ("R3", 2), ("R2a", 1), ("R2b", 1), ("R4", 2), ("R3", 1), ("Z", 3), ("R4", 1), ("Z", 2), ("Z", 1),
)


def iota(shape, dim):
    return lax.broadcasted_iota(I32, shape, dim)


def one_hot(mask):
    return jnp.where(mask, 1.0, 0.0).astype(BF16)


def dot(a, b):
    return jnp.dot(a, b, preferred_element_type=F32)


def peer_expert(place, xh, z, sign):
    step = place // 2
    half = (step + 1) // 2
    offset = half * (2 * (step % 2) - 1)
    return ((xh + place % 2) % 2) * 16 + (z + sign * offset + 16) % 16


def piece_of(slot):
    return slot - 7 * (slot >= 7).astype(I32)


def unfold(packed):
    rows = packed.shape[0]
    lane = iota((128, LANES), 1)
    spread = one_hot((iota((128, LANES), 0) - 96 == lane % 32) & (lane < FEAT))
    copies = dot(packed[:, 128:256], spread)
    slot = iota((rows, LANES), 0) % 16
    keep = (iota((rows, LANES), 1) // 32 == piece_of(slot)) & (slot < 14)
    return jnp.where(keep, copies, 0.0).astype(BF16)


def fold(spread):
    rows, width = spread.shape
    slot = iota((rows, width), 0) % 16
    keep = (iota((rows, width), 1) // 32 == piece_of(slot)) & (slot < 14)
    own = jnp.where(keep, spread, 0.0).astype(BF16)
    lane = iota((width, LANES), 1)
    gather = one_hot((lane >= FEAT) & (iota((width, LANES), 0) % 32 == lane - FEAT))
    return dot(own, gather)


def kernel(
    tokens_hbm, ids_hbm, gate_hbm, gain_hbm, w_gate, w_up, w_down, out,
    tokens, ids, gate_weight, gain,
    pack, arrived, blocks, wide, down, down_raw, hidden, core_out, core_in, sums, partial_in, x_out,
    back, returned, picks, total0, total1,
    in_sem, w_sem, z_send, z_recv, g_send, g_x, g_y, g_core, p_send, p_recv, r_send, r_recv,
    b_send, b_recv,
):
    section, expert = lax.axis_index("section"), lax.axis_index("expert")
    xl, y, core = section // 8, (section // 2) % 4, section % 2
    xh, z = expert // 16, expert % 16
    up, dn, far = (y + 1) % 4, (y + 3) % 4, (y + 2) % 4
    ox = 1 - xl
    onward, behind = jnp.where(core == 0, up, dn), jnp.where(core == 0, dn, up)

    def sec(a, b, c):
        return ((a * 4 + b) * 2 + c, expert)

    to_x, to_up, to_dn, to_core = sec(ox, y, core), sec(xl, up, core), sec(xl, dn, core), sec(xl, y, 1 - core)
    to_onward = sec(xl, onward, core)

    inputs = []
    for j, (src, dst) in enumerate(((ids_hbm, ids), (tokens_hbm, tokens), (gain_hbm, gain), (gate_hbm, gate_weight))):
        inputs.append(pltpu.make_async_copy(src, dst, in_sem.at[j]))
    loads = []
    for half, ref in enumerate((w_gate, w_up)):
        for c in range(2):
            loads.append(
                pltpu.make_async_copy(
                    ref.at[:, c],
                    wide.at[pl.ds(8 * c, 8), pl.ds(0, FEAT), pl.ds(128 * half, 128)],
                    w_sem.at[2 * half + c],
                )
            )
    loads.append(pltpu.make_async_copy(w_down, down_raw, w_sem.at[4]))
    for load in inputs + loads:
        load.start()

    barrier = pltpu.get_barrier_semaphore()
    for peer in (to_core, to_x, to_up, to_dn):
        pl.semaphore_signal(barrier, inc=1, device_id=peer, device_id_type=MESH)

    @pl.loop(1, 32)
    def _(place):
        pl.semaphore_signal(
            barrier, inc=1, device_id=(section, peer_expert(place, xh, z, 1)), device_id_type=MESH
        )

    def send(src, dst, send_sem, recv_sem, peer):
        pltpu.make_async_remote_copy(
            src_ref=src, dst_ref=dst, send_sem=send_sem, recv_sem=recv_sem, device_id=peer, device_id_type=MESH
        ).start()

    def await_bytes(ref, sem):
        pltpu.make_async_copy(ref, ref, sem).wait()

    for load in inputs:
        load.wait()
    keys = []
    named = [(iota((32, TOK), 0) == ids[k : k + 1, :]) for k in range(2)]
    before = dot(
        one_hot(named[0] | named[1]), one_hot(iota((TOK, TOK), 0) < iota((TOK, TOK), 1))
    )
    for k in range(2):
        number = jnp.sum(jnp.where(named[k], before, 0.0), axis=0, keepdims=True)
        keys.append(ids[k : k + 1, :] * 32 + number.astype(I32))
    row = iota((512, 1), 0)
    base, slot = peer_expert(row // 16, xh, z, -1) * 32, row % 16
    main_key = base + slot
    rest_key = jnp.where(slot < 14, base + 16 + (slot >= 7).astype(I32), -1)
    to_main = one_hot((keys[0] == main_key) | (keys[1] == main_key))
    to_rest = one_hot((keys[0] == rest_key) | (keys[1] == rest_key))
    widen = one_hot(iota((FEAT, LANES), 0) == iota((FEAT, LANES), 1))
    padded = dot(tokens[...], widen).astype(BF16)
    packed = dot(to_main, padded) + fold(dot(to_rest, padded))
    pack[...] = packed.astype(BF16).reshape(32, 16, LANES)
    arrived[0] = pack[0]
    gain_row = dot(jnp.broadcast_to(gain[...], (16, FEAT)), widen)[0:1, :]

    pl.semaphore_wait(barrier, 35)

    for q in SEND_ORDER:

        @pl.loop(q * PER + (1 if q == 0 else 0), q * PER + PER)
        def _(place):
            send(
                pack.at[place], arrived.at[place], z_send, z_recv.at[q],
                (section, peer_expert(place, xh, z, -1)),
            )

    def column_of(line):
        same = iota((TOK, TOK), 0) == iota((TOK, TOK), 1)
        return jnp.sum(jnp.where(same, line, jnp.zeros_like(line)), axis=1, keepdims=True)

    def prepare_mix(_):
        for k in range(2):
            key = column_of(keys[k].astype(F32)).astype(I32)
            for q in range(GROUPS):
                column = iota((1, MAIN), 1) + q * MAIN
                base, slot = peer_expert(column // 16, xh, z, -1) * 32, column % 16
                rest_key = jnp.where(slot < 14, base + 16 + (slot >= 7).astype(I32), -1)
                picks[q, 0, pl.ds(k * TOK, TOK), :] = one_hot(key == base + slot)
                picks[q, 1, pl.ds(k * TOK, TOK), :] = one_hot(key == rest_key)
        total0[...] = jnp.zeros_like(total0)
        total1[...] = jnp.zeros_like(total1)

    def prepare_weights(_):
        wide[:, FEAT:LANES, :] = jnp.zeros((16, LANES - FEAT, LANES), BF16)
        for load in loads:
            load.wait()
        for s in range(16):
            first = (s * FEAT) // 128 * 128
            shift = s * FEAT - first
            window = down_raw[:, first : min(first + 384, D)]
            place = (s % 2) * 8 + s // 2
            down[place, :, 0:FEAT] = window.astype(F32)[:, shift : shift + FEAT].astype(BF16)
            down[place, :, FEAT:LANES] = jnp.zeros((128, LANES - FEAT), BF16)

    def chip(a, b):
        return a * 4 + b

    def block(q, a, b, c):
        return blocks.at[q, c * 8 + chip(a, b)]

    def share(q, a, b, peer, recv_sem):
        ref = block(q, a, b, core)
        send(ref, ref, g_send.at[q], recv_sem, peer)

    def to_peer(q, a, b):
        share(q, a, b, to_core, g_core.at[q])

    def unpack(q):
        skip = 1 if q == 0 else 0
        await_bytes(arrived.at[pl.ds(q * PER + skip, PER - skip)], z_recv.at[q])
        got = arrived[pl.ds(q * PER, PER)].reshape(MAIN, LANES)
        lane = iota((ROWS, LANES), 1)
        row, col = iota((2 * PER, MAIN), 0), iota((2 * PER, MAIN), 1)
        slot = col % 16
        gather = one_hot((col // 16 == row // 2) & (slot < 14) & ((slot >= 7).astype(I32) == row % 2))
        rest = dot(gather, unfold(got))
        x = jnp.where(lane < FEAT, jnp.concatenate([got.astype(F32), rest], axis=0), 0.0)
        square = jnp.sum(x * x, axis=1, keepdims=True)
        high = square.astype(BF16).astype(F32)
        mid = (square - high).astype(BF16).astype(F32)
        low = square - high - mid
        x = x * gain_row
        x = jnp.where(lane == FEAT, high, x)
        x = jnp.where(lane == FEAT + 1, mid, x)
        x = jnp.where(lane == FEAT + 2, low, x)
        blocks[q, core * 8 + chip(xl, y)] = x.astype(BF16)
        share(q, xl, y, to_x, g_x.at[q, 0])
        share(q, xl, y, to_up, g_y.at[q, 0])
        share(q, xl, y, to_dn, g_y.at[q, 1])
        to_peer(q, xl, y)

    def x_then_y(q):
        await_bytes(block(q, ox, y, core), g_x.at[q, 0])
        share(q, ox, y, to_up, g_y.at[q, 2])
        share(q, ox, y, to_dn, g_y.at[q, 3])
        to_peer(q, ox, y)

    def relay_up(q):
        await_bytes(block(q, xl, dn, core), g_y.at[q, 0])
        share(q, xl, dn, to_up, g_y.at[q, 4])
        to_peer(q, xl, dn)

    def relay_dn(q):
        await_bytes(block(q, ox, up, core), g_y.at[q, 3])
        share(q, ox, up, to_dn, g_y.at[q, 5])
        to_peer(q, ox, up)

    def keep(q, a, b, sem):
        await_bytes(block(q, a, b, core), sem)
        to_peer(q, a, b)

    def y_then_x(q):
        await_bytes(block(q, xl, dn, core), g_y.at[q, 0])
        await_bytes(block(q, xl, up, core), g_y.at[q, 1])
        share(q, xl, behind, to_onward, g_y.at[q, 2])
        share(q, xl, dn, to_x, g_x.at[q, 1])
        share(q, xl, up, to_x, g_x.at[q, 2])
        to_peer(q, xl, dn)
        to_peer(q, xl, up)

    def far_then_x(q):
        await_bytes(block(q, xl, far, core), g_y.at[q, 2])
        share(q, xl, far, to_x, g_x.at[q, 3])
        to_peer(q, xl, far)

    def compute(q):
        await_bytes(blocks.at[q, pl.ds((1 - core) * 8, 8)], g_core.at[q])
        product = jnp.zeros((ROWS, LANES), F32)
        squares = jnp.zeros((ROWS, 128), F32)
        for k in range(16):
            x = blocks[q, k]
            product = product + dot(x, wide[k])
            squares = squares + x[:, 128:256].astype(F32)
        lane = iota((ROWS, 128), 1)
        kept = (lane >= FEAT - 128) & (lane < FEAT - 128 + 3)
        square = jnp.sum(jnp.where(kept, squares, 0.0), axis=1, keepdims=True)
        scale = lax.rsqrt(square * (1.0 / D) + epsilon)
        gate, upward = product[:, 0:128] * scale, product[:, 128:256] * scale
        hidden[q] = (gate / (1.0 + jnp.exp(-gate)) * upward).astype(BF16)
        for k in range(8):
            core_out[q, k] = dot(hidden[q], down[(1 - core) * 8 + k]).astype(BF16)
        send(core_out.at[q], core_in.at[q], p_send.at[q], p_recv.at[q], to_core)

    def pass_on(q, place, j, peer):
        send(sums.at[q, place], partial_in.at[q, j], r_send.at[q], r_recv.at[q, j], peer)

    def take(q, j):
        await_bytes(partial_in.at[q, j], r_recv.at[q, j])
        return partial_in[q, j].astype(F32)

    def add_core(q):
        await_bytes(core_in.at[q], p_recv.at[q])
        for k in range(8):
            own = dot(hidden[q], down[core * 8 + k])
            sums[q, k] = (own + core_in[q, k].astype(F32)).astype(BF16)
        if SCATTER_X_FIRST[q]:
            for j, b in enumerate((far, up, dn, y)):
                pass_on(q, chip(ox, b), j, to_x)
        else:
            pass_on(q, chip(xl, far), 0, to_up)
            pass_on(q, chip(ox, far), 1, to_dn)
            pass_on(q, chip(ox, up), 2, to_up)
            pass_on(q, chip(xl, dn), 3, to_dn)

    def add_into(q, place, j):
        sums[q, place] = (sums[q, place].astype(F32) + take(q, j)).astype(BF16)

    def far_up(q):
        add_into(q, chip(xl, up), 0)
        pass_on(q, chip(xl, up), 4, to_up)

    def far_dn(q):
        add_into(q, chip(ox, dn), 1)
        pass_on(q, chip(ox, dn), 5, to_dn)

    def y_sum(q):
        x_out[q] = (sums[q, chip(ox, y)].astype(F32) + take(q, 2) + take(q, 5)).astype(BF16)
        send(x_out.at[q], partial_in.at[q, 6], r_send.at[q], r_recv.at[q, 6], to_x)

    def x_far(q):
        add_into(q, chip(xl, far), 0)
        pass_on(q, chip(xl, far), 4, to_onward)

    def x_near(q):
        add_into(q, chip(xl, up), 1)
        add_into(q, chip(xl, dn), 2)
        add_into(q, chip(xl, onward), 4)
        pass_on(q, chip(xl, up), 5, to_up)
        pass_on(q, chip(xl, dn), 6, to_dn)

    def finish(q):
        total = sums[q, chip(xl, y)].astype(F32)
        for j in (3, 5, 6) if SCATTER_X_FIRST[q] else (3, 4, 6):
            total = total + take(q, j)
        row, col = iota((MAIN, 2 * PER), 0), iota((MAIN, 2 * PER), 1)
        slot = row % 16
        spread = one_hot((row // 16 == col // 2) & (slot < 14) & ((slot >= 7).astype(I32) == col % 2))
        packed = total[0:MAIN] + fold(dot(spread, total[MAIN:ROWS].astype(BF16)))
        back[pl.ds(q * PER, PER)] = packed.astype(BF16).reshape(PER, 16, LANES)
        if q == 0:
            returned[0] = back[0]

        @pl.loop(q * PER + (1 if q == 0 else 0), q * PER + PER)
        def _(place):
            send(
                back.at[place], returned.at[place], b_send, b_recv.at[q],
                (section, peer_expert(place, xh, z, 1)),
            )

    def mix(q):
        skip = 1 if q == 0 else 0
        await_bytes(returned.at[pl.ds(q * PER + skip, PER - skip)], b_recv.at[q])
        got = returned[pl.ds(q * PER, PER)].reshape(MAIN, LANES)
        picked = dot(picks[q, 0], got) + dot(picks[q, 1], unfold(got))
        total0[...] += picked[0:TOK]
        total1[...] += picked[TOK : 2 * TOK]

    tasks = {
        "W": prepare_weights, "K": prepare_mix,
        "U": unpack, "C": compute, "R1": add_core, "R4": finish, "Z": mix,
        "X": x_then_y, "Y0": relay_up, "Y1": relay_dn,
        "Y2": lambda q: keep(q, xl, up, g_y.at[q, 1]), "Y3": lambda q: keep(q, ox, dn, g_y.at[q, 2]),
        "F0": lambda q: keep(q, xl, far, g_y.at[q, 4]), "F1": lambda q: keep(q, ox, far, g_y.at[q, 5]),
        "y0": y_then_x, "f0": far_then_x,
        "x0": lambda q: keep(q, ox, y, g_x.at[q, 0]),
        "x1": lambda q: keep(q, ox, dn, g_x.at[q, 1]),
        "x2": lambda q: keep(q, ox, up, g_x.at[q, 2]),
        "x3": lambda q: keep(q, ox, far, g_x.at[q, 3]),
        "R2a": far_up, "R2b": far_dn, "R3": y_sum, "r2": x_far, "r3": x_near,
    }
    for name, q in ORDER:
        tasks[name](q)

    weights = [column_of(gate_weight[k : k + 1, :]) for k in range(2)]
    mixed = weights[0] * total0[...] + weights[1] * total1[...]
    out[...] = mixed[:, 0:FEAT].astype(BF16)

    await_bytes(pack.at[pl.ds(1, 31)], z_send)
    await_bytes(back.at[pl.ds(1, 31)], b_send)
    for q in range(GROUPS):
        await_bytes(blocks.at[q, pl.ds(0, 15)], g_send.at[q])
        await_bytes(core_out.at[q], p_send.at[q])
        await_bytes(partial_in.at[q], r_send.at[q])


def on_device(tokens, norm_gain, expert_ids, gate_weight, w_gate, w_up, w_down):
    dma = pltpu.SemaphoreType.DMA
    block = (ROWS, LANES)
    return pl.pallas_call(
        kernel,
        out_shape=jax.ShapeDtypeStruct((TOK, FEAT), BF16),
        in_specs=[pl.BlockSpec(memory_space=pl.ANY)] * 7,
        out_specs=pl.BlockSpec(memory_space=pltpu.VMEM),
        scratch_shapes=[
            pltpu.VMEM((TOK, FEAT), BF16),
            pltpu.VMEM((2, TOK), I32),
            pltpu.VMEM((2, TOK), F32),
            pltpu.VMEM((1, FEAT), BF16),
            pltpu.VMEM((32, 16, LANES), BF16),
            pltpu.VMEM((32, 16, LANES), BF16),
            pltpu.VMEM((GROUPS, 16) + block, BF16),
            pltpu.VMEM((16, LANES, LANES), BF16),
            pltpu.VMEM((16, 128, LANES), BF16),
            pltpu.VMEM((128, D), BF16),
            pltpu.VMEM((GROUPS, ROWS, 128), BF16),
            pltpu.VMEM((GROUPS, 8) + block, BF16),
            pltpu.VMEM((GROUPS, 8) + block, BF16),
            pltpu.VMEM((GROUPS, 8) + block, BF16),
            pltpu.VMEM((GROUPS, 7) + block, BF16),
            pltpu.VMEM((GROUPS,) + block, BF16),
            pltpu.VMEM((32, 16, LANES), BF16),
            pltpu.VMEM((32, 16, LANES), BF16),
            pltpu.VMEM((GROUPS, 2, 2 * TOK, MAIN), BF16),
            pltpu.VMEM((TOK, LANES), F32),
            pltpu.VMEM((TOK, LANES), F32),
            dma((4,)), dma((5,)), dma, dma((GROUPS,)),
            dma((GROUPS,)), dma((GROUPS, 4)), dma((GROUPS, 6)), dma((GROUPS,)),
            dma((GROUPS,)), dma((GROUPS,)),
            dma((GROUPS,)), dma((GROUPS, 7)),
            dma, dma((GROUPS,)),
        ],
        compiler_params=pltpu.CompilerParams(
            collective_id=0, has_side_effects=True, vmem_limit_bytes=60 * 1024 * 1024
        ),
        cost_estimate=pl.CostEstimate(flops=2_000_000_000, bytes_accessed=3_000_000, transcendentals=73728),
    )(
        tokens, expert_ids.T, gate_weight.T, norm_gain,
        w_gate.reshape(8, 2, FEAT, 128), w_up.reshape(8, 2, FEAT, 128), w_down[0],
    )


def solution(mesh):
    placed = (
        P("expert", "section"),
        P(None, "section"),
        P("expert", None),
        P("expert", None),
        P("expert", None, "section"),
        P("expert", None, "section"),
        P("expert", "section", None),
    )
    return jax.shard_map(
        on_device, mesh=mesh, in_specs=placed, out_specs=P("expert", "section"), check_vma=False
    )
```

```python
import jax
import jax.numpy as jnp
from jax import lax
from jax.experimental import pallas as pl
from jax.experimental.pallas import tpu as pltpu
from jax.sharding import PartitionSpec as P

epsilon = 1e-06
D = 3584
FEAT = 224
LANES = 256
TOK = 144
SLOTS = 16
GROUPS = 4
PER = 8
MAIN = PER * SLOTS
ROWS = MAIN + 2 * PER
F32 = jnp.float32
BF16 = jnp.bfloat16
I32 = jnp.int32
MESH = pl.DeviceIdType.MESH
SEND_ORDER = (0, 3, 2, 1)
ORDER = (
    ("K", 0), ("W", 0), ("U", 0), ("D", 0), ("D", 1), ("D", 2), ("X", 0), ("Y0", 0), ("U", 3), ("D", 3),
    ("Y1", 0), ("D", 4), ("U", 2), ("X", 3), ("D", 5), ("U", 1), ("Y0", 3), ("C1", 0), ("Y0", 2), ("D", 6),
    ("C2", 0), ("Y1", 3), ("X", 2), ("D", 7), ("Y0", 1), ("X", 1), ("C1", 3), ("Y1", 2), ("C2", 3), ("Y1", 1),
    ("R1", 0), ("C1", 2), ("R1", 3), ("C2", 2), ("C1", 1), ("R4", 0), ("C2", 1), ("R1", 2), ("R4", 3), ("Z", 0),
    ("R1", 1), ("R4", 2), ("R4", 1), ("Z", 3), ("Z", 2), ("Z", 1),
)


def iota(shape, dim):
    return lax.broadcasted_iota(I32, shape, dim)


def one_hot(mask):
    return jnp.where(mask, 1.0, 0.0).astype(BF16)


def dot(a, b):
    return jnp.dot(a, b, preferred_element_type=F32)


def peer_expert(place, xh, z, sign):
    step = place // 2
    half = (step + 1) // 2
    offset = half * (2 * (step % 2) - 1)
    return ((xh + place % 2) % 2) * 16 + (z + sign * offset + 16) % 16


def piece_of(slot):
    return slot - 7 * (slot >= 7).astype(I32)


def unfold(packed):
    rows = packed.shape[0]
    lane = iota((128, LANES), 1)
    spread = one_hot((iota((128, LANES), 0) - 96 == lane % 32) & (lane < FEAT))
    copies = dot(packed[:, 128:256], spread)
    slot = iota((rows, LANES), 0) % 16
    keep = (iota((rows, LANES), 1) // 32 == piece_of(slot)) & (slot < 14)
    return jnp.where(keep, copies, 0.0).astype(BF16)


def fold(spread):
    rows, width = spread.shape
    slot = iota((rows, width), 0) % 16
    keep = (iota((rows, width), 1) // 32 == piece_of(slot)) & (slot < 14)
    own = jnp.where(keep, spread, 0.0).astype(BF16)
    lane = iota((width, LANES), 1)
    gather = one_hot((lane >= FEAT) & (iota((width, LANES), 0) % 32 == lane - FEAT))
    return dot(own, gather)


def kernel(
    tokens_hbm, ids_hbm, gate_hbm, gain_hbm, w_gate, w_up, w_down, out,
    tokens, ids, gate_weight, gain,
    pack, arrived, blocks, wide, wide_peer, down, down_raw, down4, half_own, half_out, half_in, hidden,
    sums, partial_in, back, returned, picks, total0, total1,
    in_sem, w_sem, v_send, v_recv, d_send, d_recv, z_send, z_recv, g_send, g_x, g_y, p_send, p_recv,
    h_send, h_recv, r_send, r_recv, b_send, b_recv,
):
    section, expert = lax.axis_index("section"), lax.axis_index("expert")
    xl, y, core = section // 8, (section // 2) % 4, section % 2
    xh, z = expert // 16, expert % 16
    up, dn, far = (y + 1) % 4, (y + 3) % 4, (y + 2) % 4
    ox = 1 - xl
    corner = xl * 2 + core

    def sec(a, b, c):
        return ((a * 4 + b) * 2 + c, expert)

    to_x, to_up, to_dn, to_core = sec(ox, y, core), sec(xl, up, core), sec(xl, dn, core), sec(xl, y, 1 - core)
    to_far, to_diagonal = sec(xl, far, core), sec(ox, y, 1 - core)
    partners = ((to_core, xl, 1 - core), (to_x, ox, core), (to_diagonal, ox, 1 - core))

    inputs = []
    for j, (src, dst) in enumerate(((ids_hbm, ids), (tokens_hbm, tokens), (gain_hbm, gain), (gate_hbm, gate_weight))):
        inputs.append(pltpu.make_async_copy(src, dst, in_sem.at[j]))
    loads = []
    for half, ref in enumerate((w_gate, w_up)):
        for c in range(2):
            loads.append(
                pltpu.make_async_copy(
                    ref.at[:, c],
                    wide.at[pl.ds(8 * c, 8), pl.ds(0, FEAT), pl.ds(128 * half, 128)],
                    w_sem.at[2 * half + c],
                )
            )
    loads.append(pltpu.make_async_copy(w_down, down_raw, w_sem.at[4]))
    for load in inputs + loads:
        load.start()

    barrier = pltpu.get_barrier_semaphore()
    for peer in (to_core, to_x, to_diagonal, to_up, to_dn, to_far):
        pl.semaphore_signal(barrier, inc=1, device_id=peer, device_id_type=MESH)

    @pl.loop(1, 32)
    def _(place):
        pl.semaphore_signal(
            barrier, inc=1, device_id=(section, peer_expert(place, xh, z, 1)), device_id_type=MESH
        )

    def send(src, dst, send_sem, recv_sem, peer):
        pltpu.make_async_remote_copy(
            src_ref=src, dst_ref=dst, send_sem=send_sem, recv_sem=recv_sem, device_id=peer, device_id_type=MESH
        ).start()

    def await_bytes(ref, sem):
        pltpu.make_async_copy(ref, ref, sem).wait()

    for load in inputs:
        load.wait()
    keys = []
    named = [(iota((32, TOK), 0) == ids[k : k + 1, :]) for k in range(2)]
    before = dot(
        one_hot(named[0] | named[1]), one_hot(iota((TOK, TOK), 0) < iota((TOK, TOK), 1))
    )
    for k in range(2):
        number = jnp.sum(jnp.where(named[k], before, 0.0), axis=0, keepdims=True)
        keys.append(ids[k : k + 1, :] * 32 + number.astype(I32))
    row = iota((512, 1), 0)
    base, slot = peer_expert(row // 16, xh, z, -1) * 32, row % 16
    main_key = base + slot
    rest_key = jnp.where(slot < 14, base + 16 + (slot >= 7).astype(I32), -1)
    to_main = one_hot((keys[0] == main_key) | (keys[1] == main_key))
    to_rest = one_hot((keys[0] == rest_key) | (keys[1] == rest_key))
    widen = one_hot(iota((FEAT, LANES), 0) == iota((FEAT, LANES), 1))
    padded = dot(tokens[...], widen).astype(BF16)
    packed = dot(to_main, padded) + fold(dot(to_rest, padded))
    pack[...] = packed.astype(BF16).reshape(32, 16, LANES)
    arrived[0] = pack[0]
    gain_row = dot(jnp.broadcast_to(gain[...], (16, FEAT)), widen)[0:1, :]

    pl.semaphore_wait(barrier, 37)

    for q in SEND_ORDER:

        @pl.loop(q * PER + (1 if q == 0 else 0), q * PER + PER)
        def _(place):
            send(
                pack.at[place], arrived.at[place], z_send, z_recv.at[q],
                (section, peer_expert(place, xh, z, -1)),
            )

    def column_of(line):
        same = iota((TOK, TOK), 0) == iota((TOK, TOK), 1)
        return jnp.sum(jnp.where(same, line, jnp.zeros_like(line)), axis=1, keepdims=True)

    def prepare_mix(_):
        for k in range(2):
            key = column_of(keys[k].astype(F32)).astype(I32)
            for q in range(GROUPS):
                column = iota((1, MAIN), 1) + q * MAIN
                base, slot = peer_expert(column // 16, xh, z, -1) * 32, column % 16
                rest_key = jnp.where(slot < 14, base + 16 + (slot >= 7).astype(I32), -1)
                picks[q, 0, pl.ds(k * TOK, TOK), :] = one_hot(key == base + slot)
                picks[q, 1, pl.ds(k * TOK, TOK), :] = one_hot(key == rest_key)
        total0[...] = jnp.zeros_like(total0)
        total1[...] = jnp.zeros_like(total1)

    def prepare_weights(_):
        wide[:, FEAT:LANES, :] = jnp.zeros((16, LANES - FEAT, LANES), BF16)
        for load in loads:
            load.wait()
        send(wide.at[pl.ds((1 - core) * 8, 8)], wide_peer, v_send, v_recv, to_core)
        for s in range(16):
            first = (s * FEAT) // 128 * 128
            shift = s * FEAT - first
            window = down_raw[:, first : min(first + 384, D)]
            place = (s % 2) * 8 + s // 2
            down[place, :, 0:FEAT] = window.astype(F32)[:, shift : shift + FEAT].astype(BF16)
            down[place, :, FEAT:LANES] = jnp.zeros((128, LANES - FEAT), BF16)
        for b in range(4):
            down4[b, corner] = down[core * 8 + chip(xl, b)]
            give_down(0, b)

    def give_down(j, b):
        peer, a, c = partners[j]
        send(down.at[c * 8 + chip(a, b)], down4.at[b, corner], d_send, d_recv.at[j], peer)

    def chip(a, b):
        return a * 4 + b

    def share(q, a, b, peer, recv_sem):
        ref = blocks.at[q, chip(a, b)]
        send(ref, ref, g_send.at[q], recv_sem, peer)

    def await_block(q, a, b, sem):
        await_bytes(blocks.at[q, chip(a, b)], sem)

    def unpack(q):
        skip = 1 if q == 0 else 0
        await_bytes(arrived.at[pl.ds(q * PER + skip, PER - skip)], z_recv.at[q])
        got = arrived[pl.ds(q * PER, PER)].reshape(MAIN, LANES)
        lane = iota((ROWS, LANES), 1)
        row, col = iota((2 * PER, MAIN), 0), iota((2 * PER, MAIN), 1)
        slot = col % 16
        gather = one_hot((col // 16 == row // 2) & (slot < 14) & ((slot >= 7).astype(I32) == row % 2))
        rest = dot(gather, unfold(got))
        x = jnp.where(lane < FEAT, jnp.concatenate([got.astype(F32), rest], axis=0), 0.0)
        square = jnp.sum(x * x, axis=1, keepdims=True)
        high = square.astype(BF16).astype(F32)
        mid = (square - high).astype(BF16).astype(F32)
        low = square - high - mid
        x = x * gain_row
        x = jnp.where(lane == FEAT, high, x)
        x = jnp.where(lane == FEAT + 1, mid, x)
        x = jnp.where(lane == FEAT + 2, low, x)
        blocks[q, chip(xl, y)] = x.astype(BF16)
        share(q, xl, y, to_x, g_x.at[q])
        share(q, xl, y, to_up, g_y.at[q, 0])
        share(q, xl, y, to_dn, g_y.at[q, 1])

    def relay_x(q):
        await_block(q, ox, y, g_x.at[q])
        share(q, ox, y, to_up, g_y.at[q, 2])
        share(q, ox, y, to_dn, g_y.at[q, 3])

    def relay_up(q):
        await_block(q, xl, dn, g_y.at[q, 0])
        share(q, xl, dn, to_up, g_y.at[q, 4])

    def relay_dn(q):
        await_block(q, ox, up, g_y.at[q, 3])
        share(q, ox, up, to_dn, g_y.at[q, 5])

    waited = set()

    def once(name, wait):
        if name not in waited:
            waited.add(name)
            wait()

    def contract(q):
        await_block(q, xl, up, g_y.at[q, 1])
        await_block(q, ox, dn, g_y.at[q, 2])
        await_block(q, xl, far, g_y.at[q, 4])
        await_block(q, ox, far, g_y.at[q, 5])
        once("wide", lambda: await_bytes(wide_peer, v_recv))
        own = jnp.zeros((ROWS, LANES), F32)
        other = jnp.zeros((ROWS, LANES), F32)
        squares = jnp.zeros((ROWS, 128), F32)
        for k in range(8):
            x = blocks[q, k]
            own = own + dot(x, wide[core * 8 + k])
            other = other + dot(x, wide_peer[k])
            squares = squares + x[:, 128:256].astype(F32)
        half_out[q, :, 0:LANES] = other
        half_out[q, :, LANES : LANES + 128] = squares
        send(half_out.at[q], half_in.at[q], p_send.at[q], p_recv.at[q], to_core)
        half_own[q, :, 0:LANES] = own
        half_own[q, :, LANES : LANES + 128] = squares

    def activate(q):
        await_bytes(half_in.at[q], p_recv.at[q])
        both = half_own[q] + half_in[q]
        lane = iota((ROWS, 128), 1)
        kept = (lane >= FEAT - 128) & (lane < FEAT - 128 + 3)
        square = jnp.sum(jnp.where(kept, both[:, LANES : LANES + 128], 0.0), axis=1, keepdims=True)
        scale = lax.rsqrt(square * (1.0 / D) + epsilon)
        gate, upward = both[:, 0:128] * scale, both[:, 128:256] * scale
        hidden[q, corner] = (gate / (1.0 + jnp.exp(-gate)) * upward).astype(BF16)
        for j in (2, 1, 0):
            send(hidden.at[q, corner], hidden.at[q, corner], h_send.at[q], h_recv.at[q, j], partners[j][0])

    def spread_out(q):
        for j, (_, a, c) in enumerate(partners):
            await_bytes(hidden.at[q, a * 2 + c], h_recv.at[q, j])
            once(j, lambda: await_bytes(down4.at[:, a * 2 + c], d_recv.at[j]))
        units = jnp.concatenate([hidden[q, k] for k in range(4)], axis=1)
        for j, (b, peer) in enumerate(((far, to_far), (up, to_up), (dn, to_dn), (y, None))):
            sums[q, j] = dot(units, down4[b].reshape(512, LANES)).astype(BF16)
            if peer is not None:
                send(sums.at[q, j], partial_in.at[q, j], r_send.at[q], r_recv.at[q, j], peer)

    def finish(q):
        total = sums[q, 3].astype(F32)
        for j in (1, 2, 0):
            await_bytes(partial_in.at[q, j], r_recv.at[q, j])
            total = total + partial_in[q, j].astype(F32)
        row, col = iota((MAIN, 2 * PER), 0), iota((MAIN, 2 * PER), 1)
        slot = row % 16
        spread = one_hot((row // 16 == col // 2) & (slot < 14) & ((slot >= 7).astype(I32) == col % 2))
        packed = total[0:MAIN] + fold(dot(spread, total[MAIN:ROWS].astype(BF16)))
        back[pl.ds(q * PER, PER)] = packed.astype(BF16).reshape(PER, 16, LANES)
        if q == 0:
            returned[0] = back[0]

        @pl.loop(q * PER + (1 if q == 0 else 0), q * PER + PER)
        def _(place):
            send(
                back.at[place], returned.at[place], b_send, b_recv.at[q],
                (section, peer_expert(place, xh, z, 1)),
            )

    def mix(q):
        skip = 1 if q == 0 else 0
        await_bytes(returned.at[pl.ds(q * PER + skip, PER - skip)], b_recv.at[q])
        got = returned[pl.ds(q * PER, PER)].reshape(MAIN, LANES)
        picked = dot(picks[q, 0], got) + dot(picks[q, 1], unfold(got))
        total0[...] += picked[0:TOK]
        total1[...] += picked[TOK : 2 * TOK]

    tasks = {
        "W": prepare_weights, "K": prepare_mix,
        "U": unpack, "X": relay_x, "Y0": relay_up, "Y1": relay_dn,
        "C1": contract, "C2": activate, "R1": spread_out, "R4": finish, "Z": mix,
        "D": lambda i: give_down(2 - i % 2, i // 2),
    }
    for name, q in ORDER:
        tasks[name](q)

    weights = [column_of(gate_weight[k : k + 1, :]) for k in range(2)]
    mixed = weights[0] * total0[...] + weights[1] * total1[...]
    out[...] = mixed[:, 0:FEAT].astype(BF16)

    await_bytes(pack.at[pl.ds(1, 31)], z_send)
    await_bytes(back.at[pl.ds(1, 31)], b_send)
    await_bytes(wide_peer, v_send)
    await_bytes(down.at[pl.ds(0, 12)], d_send)
    for q in range(GROUPS):
        await_bytes(blocks.at[q, pl.ds(0, 7)], g_send.at[q])
        await_bytes(half_out.at[q], p_send.at[q])
        await_bytes(hidden.at[q, pl.ds(0, 3)], h_send.at[q])
        await_bytes(sums.at[q, pl.ds(0, 3)], r_send.at[q])


def on_device(tokens, norm_gain, expert_ids, gate_weight, w_gate, w_up, w_down):
    dma = pltpu.SemaphoreType.DMA
    block = (ROWS, LANES)
    return pl.pallas_call(
        kernel,
        out_shape=jax.ShapeDtypeStruct((TOK, FEAT), BF16),
        in_specs=[pl.BlockSpec(memory_space=pl.ANY)] * 7,
        out_specs=pl.BlockSpec(memory_space=pltpu.VMEM),
        scratch_shapes=[
            pltpu.VMEM((TOK, FEAT), BF16),
            pltpu.VMEM((2, TOK), I32),
            pltpu.VMEM((2, TOK), F32),
            pltpu.VMEM((1, FEAT), BF16),
            pltpu.VMEM((32, 16, LANES), BF16),
            pltpu.VMEM((32, 16, LANES), BF16),
            pltpu.VMEM((GROUPS, 8) + block, BF16),
            pltpu.VMEM((16, LANES, LANES), BF16),
            pltpu.VMEM((8, LANES, LANES), BF16),
            pltpu.VMEM((16, 128, LANES), BF16),
            pltpu.VMEM((128, D), BF16),
            pltpu.VMEM((4, 4, 128, LANES), BF16),
            pltpu.VMEM((GROUPS, ROWS, LANES + 128), F32),
            pltpu.VMEM((GROUPS, ROWS, LANES + 128), F32),
            pltpu.VMEM((GROUPS, ROWS, LANES + 128), F32),
            pltpu.VMEM((GROUPS, 4, ROWS, 128), BF16),
            pltpu.VMEM((GROUPS, 4) + block, BF16),
            pltpu.VMEM((GROUPS, 3) + block, BF16),
            pltpu.VMEM((32, 16, LANES), BF16),
            pltpu.VMEM((32, 16, LANES), BF16),
            pltpu.VMEM((GROUPS, 2, 2 * TOK, MAIN), BF16),
            pltpu.VMEM((TOK, LANES), F32),
            pltpu.VMEM((TOK, LANES), F32),
            dma((4,)), dma((5,)), dma, dma, dma, dma((3,)), dma, dma((GROUPS,)),
            dma((GROUPS,)), dma((GROUPS,)), dma((GROUPS, 6)), dma((GROUPS,)), dma((GROUPS,)),
            dma((GROUPS,)), dma((GROUPS, 3)), dma((GROUPS,)), dma((GROUPS, 3)), dma, dma((GROUPS,)),
        ],
        compiler_params=pltpu.CompilerParams(
            collective_id=0, has_side_effects=True, vmem_limit_bytes=60 * 1024 * 1024
        ),
        cost_estimate=pl.CostEstimate(flops=2_000_000_000, bytes_accessed=3_000_000, transcendentals=73728),
    )(
        tokens, expert_ids.T, gate_weight.T, norm_gain,
        w_gate.reshape(8, 2, FEAT, 128), w_up.reshape(8, 2, FEAT, 128), w_down[0],
    )


def solution(mesh):
    placed = (
        P("expert", "section"),
        P(None, "section"),
        P("expert", None),
        P("expert", None),
        P("expert", None, "section"),
        P("expert", None, "section"),
        P("expert", "section", None),
    )
    return jax.shard_map(
        on_device, mesh=mesh, in_specs=placed, out_specs=P("expert", "section"), check_vma=False
    )
```

```python
import jax
import jax.numpy as jnp
from jax import lax
from jax.experimental import pallas as pl
from jax.experimental.pallas import tpu as pltpu
from jax.sharding import PartitionSpec as P

epsilon = 1e-06
D = 3584
FEAT = 224
LANES = 256
TOK = 144
SLOTS = 16
GROUPS = 4
PER = 8
MAIN = PER * SLOTS
ROWS = MAIN + 2 * PER
F32 = jnp.float32
BF16 = jnp.bfloat16
I32 = jnp.int32
MESH = pl.DeviceIdType.MESH
NEAR_ORDER = (0, 1)
FAR_ORDER = (3, 2)
ORDER = (
    ("W", 0), ("K", 0), ("D", 4), ("D", 1), ("D", 6), ("S", 0), ("U", 0), ("U", 1), ("D", 5), ("D", 3),
    ("X", 0), ("D", 0), ("X", 1), ("Y1", 0), ("Y0", 1), ("Y1", 1), ("U", 3), ("Y0", 0), ("U", 2), ("C1", 1),
    ("Y0", 3), ("X", 3), ("C2", 1), ("D", 7), ("X", 2), ("Y0", 2), ("Y1", 3), ("D", 2), ("Y1", 2), ("C1", 3),
    ("R1", 1), ("C2", 3), ("C1", 2), ("C2", 2), ("R1", 3), ("R4", 1), ("C1", 0), ("R1", 2), ("C2", 0), ("R4", 3),
    ("Z", 1), ("R1", 0), ("R4", 2), ("R4", 0), ("Z", 3), ("Z", 0), ("Z", 2),
)


def iota(shape, dim):
    return lax.broadcasted_iota(I32, shape, dim)


def one_hot(mask):
    return jnp.where(mask, 1.0, 0.0).astype(BF16)


def dot(a, b):
    return jnp.dot(a, b, preferred_element_type=F32)


def peer_expert(place, xh, z, sign):
    step = place // 2
    half = (step + 1) // 2
    offset = half * (2 * (step % 2) - 1)
    return ((xh + place % 2) % 2) * 16 + (z + sign * offset + 16) % 16


def piece_of(slot):
    return slot - 7 * (slot >= 7).astype(I32)


def unfold(packed):
    rows = packed.shape[0]
    lane = iota((128, LANES), 1)
    spread = one_hot((iota((128, LANES), 0) - 96 == lane % 32) & (lane < FEAT))
    copies = dot(packed[:, 128:256], spread)
    slot = iota((rows, LANES), 0) % 16
    keep = (iota((rows, LANES), 1) // 32 == piece_of(slot)) & (slot < 14)
    return jnp.where(keep, copies, 0.0).astype(BF16)


def fold(spread):
    rows, width = spread.shape
    slot = iota((rows, width), 0) % 16
    keep = (iota((rows, width), 1) // 32 == piece_of(slot)) & (slot < 14)
    own = jnp.where(keep, spread, 0.0).astype(BF16)
    lane = iota((width, LANES), 1)
    gather = one_hot((lane >= FEAT) & (iota((width, LANES), 0) % 32 == lane - FEAT))
    return dot(own, gather)


def kernel(
    tokens_hbm, ids_hbm, gate_hbm, gain_hbm, w_gate, w_up, w_down, out,
    tokens, ids, gate_weight, gain,
    pack, arrived, blocks, wide, wide_peer, down, down_raw, down4, half_own, half_out, half_in, hidden,
    sums, partial_in, back, returned, picks, total0, total1,
    in_sem, w_sem, v_send, v_recv, d_send, d_recv, z_send, z_recv, g_send, g_x, g_y, p_send, p_recv,
    h_send, h_recv, r_send, r_recv, b_send, b_recv, near_sem,
):
    section, expert = lax.axis_index("section"), lax.axis_index("expert")
    xl, y, core = section // 8, (section // 2) % 4, section % 2
    xh, z = expert // 16, expert % 16
    up, dn, far = (y + 1) % 4, (y + 3) % 4, (y + 2) % 4
    ox = 1 - xl
    corner = xl * 2 + core

    def sec(a, b, c):
        return ((a * 4 + b) * 2 + c, expert)

    to_x, to_up, to_dn, to_core = sec(ox, y, core), sec(xl, up, core), sec(xl, dn, core), sec(xl, y, 1 - core)
    to_far, to_diagonal = sec(xl, far, core), sec(ox, y, 1 - core)
    partners = ((to_core, xl, 1 - core), (to_x, ox, core), (to_diagonal, ox, 1 - core))

    inputs = []
    for j, (src, dst) in enumerate(((ids_hbm, ids), (tokens_hbm, tokens), (gain_hbm, gain), (gate_hbm, gate_weight))):
        inputs.append(pltpu.make_async_copy(src, dst, in_sem.at[j]))
    loads = []
    for half, ref in enumerate((w_gate, w_up)):
        for c in range(2):
            loads.append(
                pltpu.make_async_copy(
                    ref.at[:, c],
                    wide.at[pl.ds(8 * c, 8), pl.ds(0, FEAT), pl.ds(128 * half, 128)],
                    w_sem.at[2 * half + c],
                )
            )
    loads.append(pltpu.make_async_copy(w_down, down_raw, w_sem.at[4]))
    for load in inputs + loads:
        load.start()

    barrier = pltpu.get_barrier_semaphore()
    for peer in (to_core, to_x, to_diagonal, to_up, to_dn, to_far):
        pl.semaphore_signal(barrier, inc=1, device_id=peer, device_id_type=MESH)

    @pl.loop(1, 18)
    def _(place):
        pl.semaphore_signal(
            barrier, inc=1, device_id=(section, peer_expert(place, xh, z, 1)), device_id_type=MESH
        )

    def send(src, dst, send_sem, recv_sem, peer):
        pltpu.make_async_remote_copy(
            src_ref=src, dst_ref=dst, send_sem=send_sem, recv_sem=recv_sem, device_id=peer, device_id_type=MESH
        ).start()

    def await_bytes(ref, sem):
        pltpu.make_async_copy(ref, ref, sem).wait()

    for load in inputs:
        load.wait()
    keys = []
    named = [(iota((32, TOK), 0) == ids[k : k + 1, :]) for k in range(2)]
    before = dot(
        one_hot(named[0] | named[1]), one_hot(iota((TOK, TOK), 0) < iota((TOK, TOK), 1))
    )
    for k in range(2):
        number = jnp.sum(jnp.where(named[k], before, 0.0), axis=0, keepdims=True)
        keys.append(ids[k : k + 1, :] * 32 + number.astype(I32))
    row = iota((512, 1), 0)
    base, slot = peer_expert(row // 16, xh, z, -1) * 32, row % 16
    main_key = base + slot
    rest_key = jnp.where(slot < 14, base + 16 + (slot >= 7).astype(I32), -1)
    to_main = one_hot((keys[0] == main_key) | (keys[1] == main_key))
    to_rest = one_hot((keys[0] == rest_key) | (keys[1] == rest_key))
    widen = one_hot(iota((FEAT, LANES), 0) == iota((FEAT, LANES), 1))
    padded = dot(tokens[...], widen).astype(BF16)
    packed = dot(to_main, padded) + fold(dot(to_rest, padded))
    pack[...] = packed.astype(BF16).reshape(32, 16, LANES)
    arrived[0] = pack[0]
    gain_row = dot(jnp.broadcast_to(gain[...], (16, FEAT)), widen)[0:1, :]

    pl.semaphore_wait(barrier, 23)
    for step in (4, 12):
        quarter = (section, xh * 16 + (z + step) % 16)
        pl.semaphore_signal(near_sem, inc=1, device_id=quarter, device_id_type=MESH)

    def dispatch(q):
        @pl.loop(q * PER + (1 if q == 0 else 0), q * PER + PER)
        def _(place):
            send(
                pack.at[place], arrived.at[place], z_send, z_recv.at[q],
                (section, peer_expert(place, xh, z, -1)),
            )

    def dispatch_far(_):
        pl.semaphore_wait(near_sem, 2)
        for q in FAR_ORDER:
            dispatch(q)

    for q in NEAR_ORDER:
        dispatch(q)

    def column_of(line):
        same = iota((TOK, TOK), 0) == iota((TOK, TOK), 1)
        return jnp.sum(jnp.where(same, line, jnp.zeros_like(line)), axis=1, keepdims=True)

    def prepare_mix(_):
        for k in range(2):
            key = column_of(keys[k].astype(F32)).astype(I32)
            for q in range(GROUPS):
                column = iota((1, MAIN), 1) + q * MAIN
                base, slot = peer_expert(column // 16, xh, z, -1) * 32, column % 16
                rest_key = jnp.where(slot < 14, base + 16 + (slot >= 7).astype(I32), -1)
                picks[q, 0, pl.ds(k * TOK, TOK), :] = one_hot(key == base + slot)
                picks[q, 1, pl.ds(k * TOK, TOK), :] = one_hot(key == rest_key)
        total0[...] = jnp.zeros_like(total0)
        total1[...] = jnp.zeros_like(total1)

    def prepare_weights(_):
        wide[:, FEAT:LANES, :] = jnp.zeros((16, LANES - FEAT, LANES), BF16)
        for load in loads:
            load.wait()
        send(wide.at[pl.ds((1 - core) * 8, 8)], wide_peer, v_send, v_recv, to_core)
        for s in range(16):
            first = (s * FEAT) // 128 * 128
            shift = s * FEAT - first
            window = down_raw[:, first : min(first + 384, D)]
            place = (s % 2) * 8 + s // 2
            down[place, :, 0:FEAT] = window.astype(F32)[:, shift : shift + FEAT].astype(BF16)
            down[place, :, FEAT:LANES] = jnp.zeros((128, LANES - FEAT), BF16)
        for b in range(4):
            down4[b, corner] = down[core * 8 + chip(xl, b)]
            give_down(0, b)

    def give_down(j, b):
        peer, a, c = partners[j]
        send(down.at[c * 8 + chip(a, b)], down4.at[b, corner], d_send, d_recv.at[j], peer)

    def chip(a, b):
        return a * 4 + b

    def share(q, a, b, peer, recv_sem):
        ref = blocks.at[q, chip(a, b)]
        send(ref, ref, g_send.at[q], recv_sem, peer)

    def await_block(q, a, b, sem):
        await_bytes(blocks.at[q, chip(a, b)], sem)

    def unpack(q):
        skip = 1 if q == 0 else 0
        await_bytes(arrived.at[pl.ds(q * PER + skip, PER - skip)], z_recv.at[q])
        got = arrived[pl.ds(q * PER, PER)].reshape(MAIN, LANES)
        lane = iota((ROWS, LANES), 1)
        row, col = iota((2 * PER, MAIN), 0), iota((2 * PER, MAIN), 1)
        slot = col % 16
        gather = one_hot((col // 16 == row // 2) & (slot < 14) & ((slot >= 7).astype(I32) == row % 2))
        rest = dot(gather, unfold(got))
        x = jnp.where(lane < FEAT, jnp.concatenate([got.astype(F32), rest], axis=0), 0.0)
        square = jnp.sum(x * x, axis=1, keepdims=True)
        high = square.astype(BF16).astype(F32)
        mid = (square - high).astype(BF16).astype(F32)
        low = square - high - mid
        x = x * gain_row
        x = jnp.where(lane == FEAT, high, x)
        x = jnp.where(lane == FEAT + 1, mid, x)
        x = jnp.where(lane == FEAT + 2, low, x)
        blocks[q, chip(xl, y)] = x.astype(BF16)
        share(q, xl, y, to_x, g_x.at[q])
        share(q, xl, y, to_up, g_y.at[q, 0])
        share(q, xl, y, to_dn, g_y.at[q, 1])

    def relay_x(q):
        await_block(q, ox, y, g_x.at[q])
        share(q, ox, y, to_up, g_y.at[q, 2])
        share(q, ox, y, to_dn, g_y.at[q, 3])

    def relay_up(q):
        await_block(q, xl, dn, g_y.at[q, 0])
        share(q, xl, dn, to_up, g_y.at[q, 4])

    def relay_dn(q):
        await_block(q, ox, up, g_y.at[q, 3])
        share(q, ox, up, to_dn, g_y.at[q, 5])

    waited = set()

    def once(name, wait):
        if name not in waited:
            waited.add(name)
            wait()

    def contract(q):
        await_block(q, xl, up, g_y.at[q, 1])
        await_block(q, ox, dn, g_y.at[q, 2])
        await_block(q, xl, far, g_y.at[q, 4])
        await_block(q, ox, far, g_y.at[q, 5])
        once("wide", lambda: await_bytes(wide_peer, v_recv))
        own = jnp.zeros((ROWS, LANES), F32)
        other = jnp.zeros((ROWS, LANES), F32)
        squares = jnp.zeros((ROWS, 128), F32)
        for k in range(8):
            x = blocks[q, k]
            own = own + dot(x, wide[core * 8 + k])
            other = other + dot(x, wide_peer[k])
            squares = squares + x[:, 128:256].astype(F32)
        half_out[q, :, 0:LANES] = other
        half_out[q, :, LANES : LANES + 128] = squares
        send(half_out.at[q], half_in.at[q], p_send.at[q], p_recv.at[q], to_core)
        half_own[q, :, 0:LANES] = own
        half_own[q, :, LANES : LANES + 128] = squares

    def activate(q):
        await_bytes(half_in.at[q], p_recv.at[q])
        both = half_own[q] + half_in[q]
        lane = iota((ROWS, 128), 1)
        kept = (lane >= FEAT - 128) & (lane < FEAT - 128 + 3)
        square = jnp.sum(jnp.where(kept, both[:, LANES : LANES + 128], 0.0), axis=1, keepdims=True)
        scale = lax.rsqrt(square * (1.0 / D) + epsilon)
        gate, upward = both[:, 0:128] * scale, both[:, 128:256] * scale
        hidden[q, corner] = (gate / (1.0 + jnp.exp(-gate)) * upward).astype(BF16)
        for j in (2, 1, 0):
            send(hidden.at[q, corner], hidden.at[q, corner], h_send.at[q], h_recv.at[q, j], partners[j][0])

    def spread_out(q):
        for j, (_, a, c) in enumerate(partners):
            await_bytes(hidden.at[q, a * 2 + c], h_recv.at[q, j])
            once(j, lambda: await_bytes(down4.at[:, a * 2 + c], d_recv.at[j]))
        units = jnp.concatenate([hidden[q, k] for k in range(4)], axis=1)
        for j, (b, peer) in enumerate(((far, to_far), (up, to_up), (dn, to_dn), (y, None))):
            sums[q, j] = dot(units, down4[b].reshape(512, LANES)).astype(BF16)
            if peer is not None:
                send(sums.at[q, j], partial_in.at[q, j], r_send.at[q], r_recv.at[q, j], peer)

    def finish(q):
        total = sums[q, 3].astype(F32)
        for j in (1, 2, 0):
            await_bytes(partial_in.at[q, j], r_recv.at[q, j])
            total = total + partial_in[q, j].astype(F32)
        row, col = iota((MAIN, 2 * PER), 0), iota((MAIN, 2 * PER), 1)
        slot = row % 16
        spread = one_hot((row // 16 == col // 2) & (slot < 14) & ((slot >= 7).astype(I32) == col % 2))
        packed = total[0:MAIN] + fold(dot(spread, total[MAIN:ROWS].astype(BF16)))
        back[pl.ds(q * PER, PER)] = packed.astype(BF16).reshape(PER, 16, LANES)
        if q == 0:
            returned[0] = back[0]

        @pl.loop(q * PER + (1 if q == 0 else 0), q * PER + PER)
        def _(place):
            send(
                back.at[place], returned.at[place], b_send, b_recv.at[q],
                (section, peer_expert(place, xh, z, 1)),
            )

    def mix(q):
        skip = 1 if q == 0 else 0
        await_bytes(returned.at[pl.ds(q * PER + skip, PER - skip)], b_recv.at[q])
        got = returned[pl.ds(q * PER, PER)].reshape(MAIN, LANES)
        picked = dot(picks[q, 0], got) + dot(picks[q, 1], unfold(got))
        total0[...] += picked[0:TOK]
        total1[...] += picked[TOK : 2 * TOK]

    tasks = {
        "S": dispatch_far, "W": prepare_weights, "K": prepare_mix,
        "U": unpack, "X": relay_x, "Y0": relay_up, "Y1": relay_dn,
        "C1": contract, "C2": activate, "R1": spread_out, "R4": finish, "Z": mix,
        "D": lambda i: give_down(2 - i % 2, i // 2),
    }
    for name, q in ORDER:
        tasks[name](q)

    weights = [column_of(gate_weight[k : k + 1, :]) for k in range(2)]
    mixed = weights[0] * total0[...] + weights[1] * total1[...]
    out[...] = mixed[:, 0:FEAT].astype(BF16)

    await_bytes(pack.at[pl.ds(1, 31)], z_send)
    await_bytes(back.at[pl.ds(1, 31)], b_send)
    await_bytes(wide_peer, v_send)
    await_bytes(down.at[pl.ds(0, 12)], d_send)
    for q in range(GROUPS):
        await_bytes(blocks.at[q, pl.ds(0, 7)], g_send.at[q])
        await_bytes(half_out.at[q], p_send.at[q])
        await_bytes(hidden.at[q, pl.ds(0, 3)], h_send.at[q])
        await_bytes(sums.at[q, pl.ds(0, 3)], r_send.at[q])


def on_device(tokens, norm_gain, expert_ids, gate_weight, w_gate, w_up, w_down):
    dma = pltpu.SemaphoreType.DMA
    block = (ROWS, LANES)
    return pl.pallas_call(
        kernel,
        out_shape=jax.ShapeDtypeStruct((TOK, FEAT), BF16),
        in_specs=[pl.BlockSpec(memory_space=pl.ANY)] * 7,
        out_specs=pl.BlockSpec(memory_space=pltpu.VMEM),
        scratch_shapes=[
            pltpu.VMEM((TOK, FEAT), BF16),
            pltpu.VMEM((2, TOK), I32),
            pltpu.VMEM((2, TOK), F32),
            pltpu.VMEM((1, FEAT), BF16),
            pltpu.VMEM((32, 16, LANES), BF16),
            pltpu.VMEM((32, 16, LANES), BF16),
            pltpu.VMEM((GROUPS, 8) + block, BF16),
            pltpu.VMEM((16, LANES, LANES), BF16),
            pltpu.VMEM((8, LANES, LANES), BF16),
            pltpu.VMEM((16, 128, LANES), BF16),
            pltpu.VMEM((128, D), BF16),
            pltpu.VMEM((4, 4, 128, LANES), BF16),
            pltpu.VMEM((GROUPS, ROWS, LANES + 128), F32),
            pltpu.VMEM((GROUPS, ROWS, LANES + 128), F32),
            pltpu.VMEM((GROUPS, ROWS, LANES + 128), F32),
            pltpu.VMEM((GROUPS, 4, ROWS, 128), BF16),
            pltpu.VMEM((GROUPS, 4) + block, BF16),
            pltpu.VMEM((GROUPS, 3) + block, BF16),
            pltpu.VMEM((32, 16, LANES), BF16),
            pltpu.VMEM((32, 16, LANES), BF16),
            pltpu.VMEM((GROUPS, 2, 2 * TOK, MAIN), BF16),
            pltpu.VMEM((TOK, LANES), F32),
            pltpu.VMEM((TOK, LANES), F32),
            dma((4,)), dma((5,)), dma, dma, dma, dma((3,)), dma, dma((GROUPS,)),
            dma((GROUPS,)), dma((GROUPS,)), dma((GROUPS, 6)), dma((GROUPS,)), dma((GROUPS,)),
            dma((GROUPS,)), dma((GROUPS, 3)), dma((GROUPS,)), dma((GROUPS, 3)), dma, dma((GROUPS,)),
            pltpu.SemaphoreType.REGULAR,
        ],
        compiler_params=pltpu.CompilerParams(
            collective_id=0, has_side_effects=True, vmem_limit_bytes=60 * 1024 * 1024
        ),
        cost_estimate=pl.CostEstimate(flops=2_000_000_000, bytes_accessed=3_000_000, transcendentals=73728),
    )(
        tokens, expert_ids.T, gate_weight.T, norm_gain,
        w_gate.reshape(8, 2, FEAT, 128), w_up.reshape(8, 2, FEAT, 128), w_down[0],
    )


def solution(mesh):
    placed = (
        P("expert", "section"),
        P(None, "section"),
        P("expert", None),
        P("expert", None),
        P("expert", None, "section"),
        P("expert", None, "section"),
        P("expert", "section", None),
    )
    return jax.shard_map(
        on_device, mesh=mesh, in_specs=placed, out_specs=P("expert", "section"), check_vma=False
    )
```

```python
import jax
import jax.numpy as jnp
from jax import lax
from jax.experimental import pallas as pl
from jax.experimental.pallas import tpu as pltpu
from jax.sharding import PartitionSpec as P

epsilon = 1e-06
D = 3584
FEAT = 224
LANES = 256
TOK = 144
SLOTS = 16
GROUPS = 4
PER = 8
MAIN = PER * SLOTS
ROWS = MAIN + 2 * PER
F32 = jnp.float32
BF16 = jnp.bfloat16
I32 = jnp.int32
MESH = pl.DeviceIdType.MESH
NEAR_ORDER = (0, 1)
FAR_ORDER = (3, 2)
FAR_RELAY = (True, True, False, False)
ORDER = (
    ("S", 0), ("W", 0), ("U", 0), ("U", 1), ("D", 3), ("X", 0), ("Y0", 0), ("D", 5), ("X", 1), ("D", 4),
    ("Y1", 0), ("Y1", 1), ("D", 0), ("Y0", 1), ("U", 3), ("D", 7), ("D", 1), ("D", 2), ("X", 3), ("C1", 1),
    ("U", 2), ("C2", 1), ("C1", 0), ("X", 2), ("D", 6), ("C2", 0), ("C1", 3), ("K", 0), ("C2", 3), ("R1", 1),
    ("C1", 2), ("R1", 3), ("C2", 2), ("R4", 1), ("R1", 2), ("R4", 3), ("Z", 1), ("R1", 0), ("R4", 2), ("R4", 0),
    ("Z", 3), ("Z", 0), ("Z", 2),
)


def iota(shape, dim):
    return lax.broadcasted_iota(I32, shape, dim)


def one_hot(mask):
    return jnp.where(mask, 1.0, 0.0).astype(BF16)


def dot(a, b):
    return jnp.dot(a, b, preferred_element_type=F32)


def peer_expert(place, xh, z, sign):
    step = place // 2
    half = (step + 1) // 2
    offset = half * (2 * (step % 2) - 1) * (1 - 2 * (place % 2))
    return ((xh + place % 2) % 2) * 16 + (z + sign * offset + 16) % 16


def piece_of(slot):
    return slot - 7 * (slot >= 7).astype(I32)


def unfold(packed):
    rows = packed.shape[0]
    lane = iota((128, LANES), 1)
    spread = one_hot((iota((128, LANES), 0) - 96 == lane % 32) & (lane < FEAT))
    copies = dot(packed[:, 128:256], spread)
    slot = iota((rows, LANES), 0) % 16
    keep = (iota((rows, LANES), 1) // 32 == piece_of(slot)) & (slot < 14)
    return jnp.where(keep, copies, 0.0).astype(BF16)


def fold(spread):
    rows, width = spread.shape
    slot = iota((rows, width), 0) % 16
    keep = (iota((rows, width), 1) // 32 == piece_of(slot)) & (slot < 14)
    own = jnp.where(keep, spread, 0.0).astype(BF16)
    lane = iota((width, LANES), 1)
    gather = one_hot((lane >= FEAT) & (iota((width, LANES), 0) % 32 == lane - FEAT))
    return dot(own, gather)


def kernel(
    tokens_hbm, ids_hbm, gate_hbm, gain_hbm, w_gate, w_up, w_down, out,
    tokens, ids, gate_weight, gain,
    pack, arrived, blocks, wide, wide_peer, down, down_raw, down4, half_own, half_out, half_in, hidden,
    sums, partial_in, back, returned, picks, total0, total1,
    in_sem, w_sem, v_send, v_recv, d_send, d_recv, z_send, z_recv, g_send, g_x, g_y, p_send, p_recv,
    h_send, h_recv, r_send, r_recv, b_send, b_recv, near_sem,
):
    section, expert = lax.axis_index("section"), lax.axis_index("expert")
    xl, y, core = section // 8, (section // 2) % 4, section % 2
    xh, z = expert // 16, expert % 16
    up, dn, far = (y + 1) % 4, (y + 3) % 4, (y + 2) % 4
    ox = 1 - xl
    corner = xl * 2 + core

    def sec(a, b, c):
        return ((a * 4 + b) * 2 + c, expert)

    to_x, to_up, to_dn, to_core = sec(ox, y, core), sec(xl, up, core), sec(xl, dn, core), sec(xl, y, 1 - core)
    to_far, to_diagonal = sec(xl, far, core), sec(ox, y, 1 - core)
    partners = ((to_core, xl, 1 - core), (to_x, ox, core), (to_diagonal, ox, 1 - core))

    inputs = []
    for j, (src, dst) in enumerate(((ids_hbm, ids), (tokens_hbm, tokens), (gain_hbm, gain), (gate_hbm, gate_weight))):
        inputs.append(pltpu.make_async_copy(src, dst, in_sem.at[j]))
    loads = []
    for half, ref in enumerate((w_gate, w_up)):
        for c in range(2):
            loads.append(
                pltpu.make_async_copy(
                    ref.at[:, c],
                    wide.at[pl.ds(8 * c, 8), pl.ds(0, FEAT), pl.ds(128 * half, 128)],
                    w_sem.at[2 * half + c],
                )
            )
    loads.append(pltpu.make_async_copy(w_down, down_raw, w_sem.at[4]))
    for load in inputs + loads:
        load.start()

    barrier = pltpu.get_barrier_semaphore()
    for peer in (to_core, to_x, to_diagonal, to_up, to_dn, to_far):
        pl.semaphore_signal(barrier, inc=1, device_id=peer, device_id_type=MESH)

    @pl.loop(1, 18)
    def _(place):
        pl.semaphore_signal(
            barrier, inc=1, device_id=(section, peer_expert(place, xh, z, 1)), device_id_type=MESH
        )

    def send(src, dst, send_sem, recv_sem, peer):
        pltpu.make_async_remote_copy(
            src_ref=src, dst_ref=dst, send_sem=send_sem, recv_sem=recv_sem, device_id=peer, device_id_type=MESH
        ).start()

    def await_bytes(ref, sem):
        pltpu.make_async_copy(ref, ref, sem).wait()

    for load in inputs:
        load.wait()
    keys = []
    named = [(iota((32, TOK), 0) == ids[k : k + 1, :]) for k in range(2)]
    before = dot(
        one_hot(named[0] | named[1]), one_hot(iota((TOK, TOK), 0) < iota((TOK, TOK), 1))
    )
    for k in range(2):
        number = jnp.sum(jnp.where(named[k], before, 0.0), axis=0, keepdims=True)
        keys.append(ids[k : k + 1, :] * 32 + number.astype(I32))
    row = iota((512, 1), 0)
    base, slot = peer_expert(row // 16, xh, z, -1) * 32, row % 16
    main_key = base + slot
    rest_key = jnp.where(slot < 14, base + 16 + (slot >= 7).astype(I32), -1)
    to_main = one_hot((keys[0] == main_key) | (keys[1] == main_key))
    to_rest = one_hot((keys[0] == rest_key) | (keys[1] == rest_key))
    widen = one_hot(iota((FEAT, LANES), 0) == iota((FEAT, LANES), 1))
    padded = dot(tokens[...], widen).astype(BF16)
    packed = dot(to_main, padded) + fold(dot(to_rest, padded))
    pack[...] = packed.astype(BF16).reshape(32, 16, LANES)
    arrived[0] = pack[0]
    gain_row = dot(jnp.broadcast_to(gain[...], (16, FEAT)), widen)[0:1, :]

    pl.semaphore_wait(barrier, 23)
    for step in (4, 12):
        quarter = (section, xh * 16 + (z + step) % 16)
        pl.semaphore_signal(near_sem, inc=1, device_id=quarter, device_id_type=MESH)

    def dispatch(q):
        @pl.loop(q * PER + (1 if q == 0 else 0), q * PER + PER)
        def _(place):
            send(
                pack.at[place], arrived.at[place], z_send, z_recv.at[q],
                (section, peer_expert(place, xh, z, -1)),
            )

    def dispatch_far(_):
        pl.semaphore_wait(near_sem, 2)
        for q in FAR_ORDER:
            dispatch(q)

    for q in NEAR_ORDER:
        dispatch(q)

    def column_of(line):
        same = iota((TOK, TOK), 0) == iota((TOK, TOK), 1)
        return jnp.sum(jnp.where(same, line, jnp.zeros_like(line)), axis=1, keepdims=True)

    def prepare_mix(_):
        for k in range(2):
            key = column_of(keys[k].astype(F32)).astype(I32)
            for q in range(GROUPS):
                column = iota((1, MAIN), 1) + q * MAIN
                base, slot = peer_expert(column // 16, xh, z, -1) * 32, column % 16
                rest_key = jnp.where(slot < 14, base + 16 + (slot >= 7).astype(I32), -1)
                picks[q, 0, pl.ds(k * TOK, TOK), :] = one_hot(key == base + slot)
                picks[q, 1, pl.ds(k * TOK, TOK), :] = one_hot(key == rest_key)
        total0[...] = jnp.zeros_like(total0)
        total1[...] = jnp.zeros_like(total1)

    def prepare_weights(_):
        wide[:, FEAT:LANES, :] = jnp.zeros((16, LANES - FEAT, LANES), BF16)
        for load in loads:
            load.wait()
        send(wide.at[pl.ds((1 - core) * 8, 8)], wide_peer, v_send, v_recv, to_core)
        for s in range(16):
            first = (s * FEAT) // 128 * 128
            shift = s * FEAT - first
            window = down_raw[:, first : min(first + 384, D)]
            place = (s % 2) * 8 + s // 2
            down[place, :, 0:FEAT] = window.astype(F32)[:, shift : shift + FEAT].astype(BF16)
            down[place, :, FEAT:LANES] = jnp.zeros((128, LANES - FEAT), BF16)
        for b in range(4):
            down4[b, corner] = down[core * 8 + chip(xl, b)]
            give_down(0, b)

    def give_down(j, b):
        peer, a, c = partners[j]
        send(down.at[c * 8 + chip(a, b)], down4.at[b, corner], d_send, d_recv.at[j], peer)

    def chip(a, b):
        return a * 4 + b

    def share(q, a, b, peer, recv_sem):
        ref = blocks.at[q, chip(a, b)]
        send(ref, ref, g_send.at[q], recv_sem, peer)

    def await_block(q, a, b, sem):
        await_bytes(blocks.at[q, chip(a, b)], sem)

    def unpack(q):
        skip = 1 if q == 0 else 0
        await_bytes(arrived.at[pl.ds(q * PER + skip, PER - skip)], z_recv.at[q])
        got = arrived[pl.ds(q * PER, PER)].reshape(MAIN, LANES)
        lane = iota((ROWS, LANES), 1)
        row, col = iota((2 * PER, MAIN), 0), iota((2 * PER, MAIN), 1)
        slot = col % 16
        gather = one_hot((col // 16 == row // 2) & (slot < 14) & ((slot >= 7).astype(I32) == row % 2))
        rest = dot(gather, unfold(got))
        x = jnp.where(lane < FEAT, jnp.concatenate([got.astype(F32), rest], axis=0), 0.0)
        square = jnp.sum(x * x, axis=1, keepdims=True)
        high = square.astype(BF16).astype(F32)
        mid = (square - high).astype(BF16).astype(F32)
        low = square - high - mid
        x = x * gain_row
        x = jnp.where(lane == FEAT, high, x)
        x = jnp.where(lane == FEAT + 1, mid, x)
        x = jnp.where(lane == FEAT + 2, low, x)
        blocks[q, chip(xl, y)] = x.astype(BF16)
        share(q, xl, y, to_x, g_x.at[q])
        share(q, xl, y, to_up, g_y.at[q, 0])
        share(q, xl, y, to_dn, g_y.at[q, 1])
        if not FAR_RELAY[q]:
            share(q, xl, y, to_far, g_y.at[q, 4])

    def relay_x(q):
        await_block(q, ox, y, g_x.at[q])
        share(q, ox, y, to_up, g_y.at[q, 2])
        share(q, ox, y, to_dn, g_y.at[q, 3])
        if not FAR_RELAY[q]:
            share(q, ox, y, to_far, g_y.at[q, 5])

    def relay_up(q):
        await_block(q, xl, dn, g_y.at[q, 0])
        share(q, xl, dn, to_up, g_y.at[q, 4])

    def relay_dn(q):
        await_block(q, ox, up, g_y.at[q, 3])
        share(q, ox, up, to_dn, g_y.at[q, 5])

    waited = set()

    def once(name, wait):
        if name not in waited:
            waited.add(name)
            wait()

    def contract(q):
        if not FAR_RELAY[q]:
            await_block(q, xl, dn, g_y.at[q, 0])
            await_block(q, ox, up, g_y.at[q, 3])
        await_block(q, xl, up, g_y.at[q, 1])
        await_block(q, ox, dn, g_y.at[q, 2])
        await_block(q, xl, far, g_y.at[q, 4])
        await_block(q, ox, far, g_y.at[q, 5])
        once("wide", lambda: await_bytes(wide_peer, v_recv))
        own = jnp.zeros((ROWS, LANES), F32)
        other = jnp.zeros((ROWS, LANES), F32)
        squares = jnp.zeros((ROWS, 128), F32)
        for k in range(8):
            x = blocks[q, k]
            own = own + dot(x, wide[core * 8 + k])
            other = other + dot(x, wide_peer[k])
            squares = squares + x[:, 128:256].astype(F32)
        half_out[q, :, 0:LANES] = other
        half_out[q, :, LANES : LANES + 128] = squares
        send(half_out.at[q], half_in.at[q], p_send.at[q], p_recv.at[q], to_core)
        half_own[q, :, 0:LANES] = own
        half_own[q, :, LANES : LANES + 128] = squares

    def activate(q):
        await_bytes(half_in.at[q], p_recv.at[q])
        both = half_own[q] + half_in[q]
        lane = iota((ROWS, 128), 1)
        kept = (lane >= FEAT - 128) & (lane < FEAT - 128 + 3)
        square = jnp.sum(jnp.where(kept, both[:, LANES : LANES + 128], 0.0), axis=1, keepdims=True)
        scale = lax.rsqrt(square * (1.0 / D) + epsilon)
        gate, upward = both[:, 0:128] * scale, both[:, 128:256] * scale
        hidden[q, corner] = (gate / (1.0 + jnp.exp(-gate)) * upward).astype(BF16)
        for j in (2, 1, 0):
            send(hidden.at[q, corner], hidden.at[q, corner], h_send.at[q], h_recv.at[q, j], partners[j][0])

    def spread_out(q):
        for j, (_, a, c) in enumerate(partners):
            await_bytes(hidden.at[q, a * 2 + c], h_recv.at[q, j])
            once(j, lambda: await_bytes(down4.at[:, a * 2 + c], d_recv.at[j]))
        units = jnp.concatenate([hidden[q, k] for k in range(4)], axis=1)
        for j, (b, peer) in enumerate(((far, to_far), (up, to_up), (dn, to_dn), (y, None))):
            sums[q, j] = dot(units, down4[b].reshape(512, LANES)).astype(BF16)
            if peer is not None:
                send(sums.at[q, j], partial_in.at[q, j], r_send.at[q], r_recv.at[q, j], peer)

    def finish(q):
        total = sums[q, 3].astype(F32)
        for j in (1, 2, 0):
            await_bytes(partial_in.at[q, j], r_recv.at[q, j])
            total = total + partial_in[q, j].astype(F32)
        row, col = iota((MAIN, 2 * PER), 0), iota((MAIN, 2 * PER), 1)
        slot = row % 16
        spread = one_hot((row // 16 == col // 2) & (slot < 14) & ((slot >= 7).astype(I32) == col % 2))
        packed = total[0:MAIN] + fold(dot(spread, total[MAIN:ROWS].astype(BF16)))
        back[pl.ds(q * PER, PER)] = packed.astype(BF16).reshape(PER, 16, LANES)
        if q == 0:
            returned[0] = back[0]

        @pl.loop(q * PER + (1 if q == 0 else 0), q * PER + PER)
        def _(place):
            send(
                back.at[place], returned.at[place], b_send, b_recv.at[q],
                (section, peer_expert(place, xh, z, 1)),
            )

    def mix(q):
        skip = 1 if q == 0 else 0
        await_bytes(returned.at[pl.ds(q * PER + skip, PER - skip)], b_recv.at[q])
        got = returned[pl.ds(q * PER, PER)].reshape(MAIN, LANES)
        picked = dot(picks[q, 0], got) + dot(picks[q, 1], unfold(got))
        total0[...] += picked[0:TOK]
        total1[...] += picked[TOK : 2 * TOK]

    tasks = {
        "S": dispatch_far, "W": prepare_weights, "K": prepare_mix,
        "U": unpack, "X": relay_x, "Y0": relay_up, "Y1": relay_dn,
        "C1": contract, "C2": activate, "R1": spread_out, "R4": finish, "Z": mix,
        "D": lambda i: give_down(2 - i % 2, i // 2),
    }
    for name, q in ORDER:
        tasks[name](q)

    weights = [column_of(gate_weight[k : k + 1, :]) for k in range(2)]
    mixed = weights[0] * total0[...] + weights[1] * total1[...]
    out[...] = mixed[:, 0:FEAT].astype(BF16)

    await_bytes(pack.at[pl.ds(1, 31)], z_send)
    await_bytes(back.at[pl.ds(1, 31)], b_send)
    await_bytes(wide_peer, v_send)
    await_bytes(down.at[pl.ds(0, 12)], d_send)
    for q in range(GROUPS):
        await_bytes(blocks.at[q, pl.ds(0, 7)], g_send.at[q])
        await_bytes(half_out.at[q], p_send.at[q])
        await_bytes(hidden.at[q, pl.ds(0, 3)], h_send.at[q])
        await_bytes(sums.at[q, pl.ds(0, 3)], r_send.at[q])


def on_device(tokens, norm_gain, expert_ids, gate_weight, w_gate, w_up, w_down):
    dma = pltpu.SemaphoreType.DMA
    block = (ROWS, LANES)
    return pl.pallas_call(
        kernel,
        out_shape=jax.ShapeDtypeStruct((TOK, FEAT), BF16),
        in_specs=[pl.BlockSpec(memory_space=pl.ANY)] * 7,
        out_specs=pl.BlockSpec(memory_space=pltpu.VMEM),
        scratch_shapes=[
            pltpu.VMEM((TOK, FEAT), BF16),
            pltpu.VMEM((2, TOK), I32),
            pltpu.VMEM((2, TOK), F32),
            pltpu.VMEM((1, FEAT), BF16),
            pltpu.VMEM((32, 16, LANES), BF16),
            pltpu.VMEM((32, 16, LANES), BF16),
            pltpu.VMEM((GROUPS, 8) + block, BF16),
            pltpu.VMEM((16, LANES, LANES), BF16),
            pltpu.VMEM((8, LANES, LANES), BF16),
            pltpu.VMEM((16, 128, LANES), BF16),
            pltpu.VMEM((128, D), BF16),
            pltpu.VMEM((4, 4, 128, LANES), BF16),
            pltpu.VMEM((GROUPS, ROWS, LANES + 128), F32),
            pltpu.VMEM((GROUPS, ROWS, LANES + 128), F32),
            pltpu.VMEM((GROUPS, ROWS, LANES + 128), F32),
            pltpu.VMEM((GROUPS, 4, ROWS, 128), BF16),
            pltpu.VMEM((GROUPS, 4) + block, BF16),
            pltpu.VMEM((GROUPS, 3) + block, BF16),
            pltpu.VMEM((32, 16, LANES), BF16),
            pltpu.VMEM((32, 16, LANES), BF16),
            pltpu.VMEM((GROUPS, 2, 2 * TOK, MAIN), BF16),
            pltpu.VMEM((TOK, LANES), F32),
            pltpu.VMEM((TOK, LANES), F32),
            dma((4,)), dma((5,)), dma, dma, dma, dma((3,)), dma, dma((GROUPS,)),
            dma((GROUPS,)), dma((GROUPS,)), dma((GROUPS, 6)), dma((GROUPS,)), dma((GROUPS,)),
            dma((GROUPS,)), dma((GROUPS, 3)), dma((GROUPS,)), dma((GROUPS, 3)), dma, dma((GROUPS,)),
            pltpu.SemaphoreType.REGULAR,
        ],
        compiler_params=pltpu.CompilerParams(
            collective_id=0, has_side_effects=True, vmem_limit_bytes=60 * 1024 * 1024
        ),
        cost_estimate=pl.CostEstimate(flops=2_000_000_000, bytes_accessed=3_000_000, transcendentals=73728),
    )(
        tokens, expert_ids.T, gate_weight.T, norm_gain,
        w_gate.reshape(8, 2, FEAT, 128), w_up.reshape(8, 2, FEAT, 128), w_down[0],
    )


def solution(mesh):
    placed = (
        P("expert", "section"),
        P(None, "section"),
        P("expert", None),
        P("expert", None),
        P("expert", None, "section"),
        P("expert", None, "section"),
        P("expert", "section", None),
    )
    return jax.shard_map(
        on_device, mesh=mesh, in_specs=placed, out_specs=P("expert", "section"), check_vma=False
    )
```

```python
import jax
import jax.numpy as jnp
from jax import lax
from jax.experimental import pallas as pl
from jax.experimental.pallas import tpu as pltpu
from jax.sharding import PartitionSpec as P

epsilon = 1e-06
D = 3584
FEAT = 224
LANES = 256
TOK = 144
SLOTS = 16
GROUPS = 4
PER = 8
MAIN = PER * SLOTS
ROWS = MAIN + 2 * PER
F32 = jnp.float32
BF16 = jnp.bfloat16
I32 = jnp.int32
MESH = pl.DeviceIdType.MESH
NEAR_ORDER = (0, 1)
FAR_ORDER = (3, 2)
MODES = "xxXX"
ORDER = (
    ("W", 0), ("S", 3), ("U", 0), ("U", 1), ("D", 3), ("X", 0), ("Y0", 0), ("D", 5), ("X", 1), ("S", 2),
    ("D", 4), ("Y1", 0), ("Y1", 1), ("D", 0), ("Y0", 1), ("U", 3), ("D", 7), ("D", 1), ("D", 2), ("X", 3),
    ("C1", 1), ("U", 2), ("C2", 1), ("C1", 0), ("X", 2), ("D", 6), ("C2", 0), ("C1", 3), ("K", 0), ("C2", 3),
    ("R1", 1), ("C1", 2), ("R1", 3), ("C2", 2), ("R4", 1), ("R1", 2), ("R4", 3), ("Z", 1), ("R1", 0), ("R4", 2),
    ("R4", 0), ("Z", 3), ("Z", 0), ("Z", 2),
)


def iota(shape, dim):
    return lax.broadcasted_iota(I32, shape, dim)


def one_hot(mask):
    return jnp.where(mask, 1.0, 0.0).astype(BF16)


def dot(a, b):
    return jnp.dot(a, b, preferred_element_type=F32)


def peer_expert(place, xh, z, sign):
    step = place // 2
    half = (step + 1) // 2
    offset = half * (2 * (step % 2) - 1) * (1 - 2 * (place % 2))
    return ((xh + place % 2) % 2) * 16 + (z + sign * offset + 16) % 16


def piece_of(slot):
    return slot - 7 * (slot >= 7).astype(I32)


def unfold(packed):
    rows = packed.shape[0]
    lane = iota((128, LANES), 1)
    spread = one_hot((iota((128, LANES), 0) - 96 == lane % 32) & (lane < FEAT))
    copies = dot(packed[:, 128:256], spread)
    slot = iota((rows, LANES), 0) % 16
    keep = (iota((rows, LANES), 1) // 32 == piece_of(slot)) & (slot < 14)
    return jnp.where(keep, copies, 0.0).astype(BF16)


def fold(spread):
    rows, width = spread.shape
    slot = iota((rows, width), 0) % 16
    keep = (iota((rows, width), 1) // 32 == piece_of(slot)) & (slot < 14)
    own = jnp.where(keep, spread, 0.0).astype(BF16)
    lane = iota((width, LANES), 1)
    gather = one_hot((lane >= FEAT) & (iota((width, LANES), 0) % 32 == lane - FEAT))
    return dot(own, gather)


def kernel(
    tokens_hbm, ids_hbm, gate_hbm, gain_hbm, w_gate, w_up, w_down, out,
    tokens, ids, gate_weight, gain,
    pack, arrived, blocks, wide, wide_peer, down, down_raw, down4, half_own, half_out, half_in, hidden,
    sums, partial_in, back, returned, picks, total0, total1,
    in_sem, w_sem, v_send, v_recv, d_send, d_recv, z_send, z_recv, g_send, g_x, g_y, p_send, p_recv,
    h_send, h_recv, r_send, r_recv, b_send, b_recv, near_sem,
):
    section, expert = lax.axis_index("section"), lax.axis_index("expert")
    xl, y, core = section // 8, (section // 2) % 4, section % 2
    xh, z = expert // 16, expert % 16
    up, dn, far = (y + 1) % 4, (y + 3) % 4, (y + 2) % 4
    ox = 1 - xl
    corner = xl * 2 + core

    def sec(a, b, c):
        return ((a * 4 + b) * 2 + c, expert)

    to_x, to_up, to_dn, to_core = sec(ox, y, core), sec(xl, up, core), sec(xl, dn, core), sec(xl, y, 1 - core)
    to_far, to_diagonal = sec(xl, far, core), sec(ox, y, 1 - core)
    partners = ((to_core, xl, 1 - core), (to_x, ox, core), (to_diagonal, ox, 1 - core))

    inputs = []
    for j, (src, dst) in enumerate(((ids_hbm, ids), (tokens_hbm, tokens), (gain_hbm, gain), (gate_hbm, gate_weight))):
        inputs.append(pltpu.make_async_copy(src, dst, in_sem.at[j]))
    loads = []
    for half, ref in enumerate((w_gate, w_up)):
        for c in range(2):
            loads.append(
                pltpu.make_async_copy(
                    ref.at[:, c],
                    wide.at[pl.ds(8 * c, 8), pl.ds(0, FEAT), pl.ds(128 * half, 128)],
                    w_sem.at[2 * half + c],
                )
            )
    loads.append(pltpu.make_async_copy(w_down, down_raw, w_sem.at[4]))
    for load in inputs + loads:
        load.start()

    barrier = pltpu.get_barrier_semaphore()
    for peer in (to_core, to_x, to_diagonal, to_up, to_dn, to_far):
        pl.semaphore_signal(barrier, inc=1, device_id=peer, device_id_type=MESH)

    @pl.loop(1, 18)
    def _(place):
        pl.semaphore_signal(
            barrier, inc=1, device_id=(section, peer_expert(place, xh, z, 1)), device_id_type=MESH
        )

    def send(src, dst, send_sem, recv_sem, peer):
        pltpu.make_async_remote_copy(
            src_ref=src, dst_ref=dst, send_sem=send_sem, recv_sem=recv_sem, device_id=peer, device_id_type=MESH
        ).start()

    def await_bytes(ref, sem):
        pltpu.make_async_copy(ref, ref, sem).wait()

    for load in inputs:
        load.wait()
    keys = []
    named = [(iota((32, TOK), 0) == ids[k : k + 1, :]) for k in range(2)]
    before = dot(
        one_hot(named[0] | named[1]), one_hot(iota((TOK, TOK), 0) < iota((TOK, TOK), 1))
    )
    for k in range(2):
        number = jnp.sum(jnp.where(named[k], before, 0.0), axis=0, keepdims=True)
        keys.append(ids[k : k + 1, :] * 32 + number.astype(I32))
    row = iota((512, 1), 0)
    base, slot = peer_expert(row // 16, xh, z, -1) * 32, row % 16
    main_key = base + slot
    rest_key = jnp.where(slot < 14, base + 16 + (slot >= 7).astype(I32), -1)
    to_main = one_hot((keys[0] == main_key) | (keys[1] == main_key))
    to_rest = one_hot((keys[0] == rest_key) | (keys[1] == rest_key))
    widen = one_hot(iota((FEAT, LANES), 0) == iota((FEAT, LANES), 1))
    padded = dot(tokens[...], widen).astype(BF16)
    packed = dot(to_main, padded) + fold(dot(to_rest, padded))
    pack[...] = packed.astype(BF16).reshape(32, 16, LANES)
    arrived[0] = pack[0]
    gain_row = dot(jnp.broadcast_to(gain[...], (16, FEAT)), widen)[0:1, :]

    pl.semaphore_wait(barrier, 23)
    for step in (4, 12):
        quarter = (section, xh * 16 + (z + step) % 16)
        pl.semaphore_signal(near_sem, inc=1, device_id=quarter, device_id_type=MESH)

    def dispatch(q):
        @pl.loop(q * PER + (1 if q == 0 else 0), q * PER + PER)
        def _(place):
            send(
                pack.at[place], arrived.at[place], z_send, z_recv.at[q],
                (section, peer_expert(place, xh, z, -1)),
            )

    def dispatch_far(q):
        if q == FAR_ORDER[0]:
            pl.semaphore_wait(near_sem, 2)
        dispatch(q)

    for q in NEAR_ORDER:
        dispatch(q)

    def column_of(line):
        same = iota((TOK, TOK), 0) == iota((TOK, TOK), 1)
        return jnp.sum(jnp.where(same, line, jnp.zeros_like(line)), axis=1, keepdims=True)

    def prepare_mix(_):
        for k in range(2):
            key = column_of(keys[k].astype(F32)).astype(I32)
            for q in range(GROUPS):
                column = iota((1, MAIN), 1) + q * MAIN
                base, slot = peer_expert(column // 16, xh, z, -1) * 32, column % 16
                rest_key = jnp.where(slot < 14, base + 16 + (slot >= 7).astype(I32), -1)
                picks[q, 0, pl.ds(k * TOK, TOK), :] = one_hot(key == base + slot)
                picks[q, 1, pl.ds(k * TOK, TOK), :] = one_hot(key == rest_key)
        total0[...] = jnp.zeros_like(total0)
        total1[...] = jnp.zeros_like(total1)

    def prepare_weights(_):
        wide[:, FEAT:LANES, :] = jnp.zeros((16, LANES - FEAT, LANES), BF16)
        for load in loads:
            load.wait()
        send(wide.at[pl.ds((1 - core) * 8, 8)], wide_peer, v_send, v_recv, to_core)
        for s in range(16):
            first = (s * FEAT) // 128 * 128
            shift = s * FEAT - first
            window = down_raw[:, first : min(first + 384, D)]
            place = (s % 2) * 8 + s // 2
            down[place, :, 0:FEAT] = window.astype(F32)[:, shift : shift + FEAT].astype(BF16)
            down[place, :, FEAT:LANES] = jnp.zeros((128, LANES - FEAT), BF16)
        for b in range(4):
            down4[b, corner] = down[core * 8 + chip(xl, b)]
            give_down(0, b)

    def give_down(j, b):
        peer, a, c = partners[j]
        send(down.at[c * 8 + chip(a, b)], down4.at[b, corner], d_send, d_recv.at[j], peer)

    def chip(a, b):
        return a * 4 + b

    def share(q, a, b, peer, recv_sem):
        ref = blocks.at[q, chip(a, b)]
        send(ref, ref, g_send.at[q], recv_sem, peer)

    def await_block(q, a, b, sem):
        await_bytes(blocks.at[q, chip(a, b)], sem)

    def unpack(q):
        skip = 1 if q == 0 else 0
        await_bytes(arrived.at[pl.ds(q * PER + skip, PER - skip)], z_recv.at[q])
        got = arrived[pl.ds(q * PER, PER)].reshape(MAIN, LANES)
        lane = iota((ROWS, LANES), 1)
        row, col = iota((2 * PER, MAIN), 0), iota((2 * PER, MAIN), 1)
        slot = col % 16
        gather = one_hot((col // 16 == row // 2) & (slot < 14) & ((slot >= 7).astype(I32) == row % 2))
        rest = dot(gather, unfold(got))
        x = jnp.where(lane < FEAT, jnp.concatenate([got.astype(F32), rest], axis=0), 0.0)
        square = jnp.sum(x * x, axis=1, keepdims=True)
        high = square.astype(BF16).astype(F32)
        mid = (square - high).astype(BF16).astype(F32)
        low = square - high - mid
        x = x * gain_row
        x = jnp.where(lane == FEAT, high, x)
        x = jnp.where(lane == FEAT + 1, mid, x)
        x = jnp.where(lane == FEAT + 2, low, x)
        blocks[q, chip(xl, y)] = x.astype(BF16)
        share(q, xl, y, to_x, g_x.at[q])
        share(q, xl, y, to_up, g_y.at[q, 0])
        share(q, xl, y, to_dn, g_y.at[q, 1])
        if MODES[q] != "x":
            share(q, xl, y, to_far, g_y.at[q, 4])

    def relay_to_y(q):
        await_block(q, ox, y, g_x.at[q])
        share(q, ox, y, to_up, g_y.at[q, 2])
        share(q, ox, y, to_dn, g_y.at[q, 3])
        if MODES[q] != "x":
            share(q, ox, y, to_far, g_y.at[q, 5])

    def relay_to_x(q):
        for j, (b, onward) in enumerate(((dn, 2), (up, 3), (far, 5))):
            await_block(q, xl, b, g_y.at[q, (0, 1, 4)[j]])
            share(q, xl, b, to_x, g_y.at[q, onward])

    def await_column(q):
        for b, sem in ((dn, 0), (up, 1), (far, 4)):
            await_block(q, xl, b, g_y.at[q, sem])

    def by_core(first, second):
        pl.when(core == 0)(first)
        pl.when(core == 1)(second)

    def relay(q):
        if MODES[q] == "M":
            by_core(lambda: relay_to_y(q), lambda: relay_to_x(q))
        else:
            relay_to_y(q)

    def relay_up(q):
        await_block(q, xl, dn, g_y.at[q, 0])
        share(q, xl, dn, to_up, g_y.at[q, 4])

    def relay_dn(q):
        await_block(q, ox, up, g_y.at[q, 3])
        share(q, ox, up, to_dn, g_y.at[q, 5])

    waited = set()

    def once(name, wait):
        if name not in waited:
            waited.add(name)
            wait()

    def contract(q):
        if MODES[q] == "x":
            await_block(q, xl, up, g_y.at[q, 1])
            await_block(q, ox, dn, g_y.at[q, 2])
            await_block(q, xl, far, g_y.at[q, 4])
        else:
            if MODES[q] == "X":
                await_column(q)
            else:
                by_core(lambda: await_column(q), lambda: await_block(q, ox, y, g_x.at[q]))
            await_block(q, ox, dn, g_y.at[q, 2])
            await_block(q, ox, up, g_y.at[q, 3])
        await_block(q, ox, far, g_y.at[q, 5])
        once("wide", lambda: await_bytes(wide_peer, v_recv))
        own = jnp.zeros((ROWS, LANES), F32)
        other = jnp.zeros((ROWS, LANES), F32)
        squares = jnp.zeros((ROWS, 128), F32)
        for k in range(8):
            x = blocks[q, k]
            own = own + dot(x, wide[core * 8 + k])
            other = other + dot(x, wide_peer[k])
            squares = squares + x[:, 128:256].astype(F32)
        half_out[q, :, 0:LANES] = other
        half_out[q, :, LANES : LANES + 128] = squares
        send(half_out.at[q], half_in.at[q], p_send.at[q], p_recv.at[q], to_core)
        half_own[q, :, 0:LANES] = own
        half_own[q, :, LANES : LANES + 128] = squares

    def activate(q):
        await_bytes(half_in.at[q], p_recv.at[q])
        both = half_own[q] + half_in[q]
        lane = iota((ROWS, 128), 1)
        kept = (lane >= FEAT - 128) & (lane < FEAT - 128 + 3)
        square = jnp.sum(jnp.where(kept, both[:, LANES : LANES + 128], 0.0), axis=1, keepdims=True)
        scale = lax.rsqrt(square * (1.0 / D) + epsilon)
        gate, upward = both[:, 0:128] * scale, both[:, 128:256] * scale
        hidden[q, corner] = (gate / (1.0 + jnp.exp(-gate)) * upward).astype(BF16)
        for j in (2, 1, 0):
            send(hidden.at[q, corner], hidden.at[q, corner], h_send.at[q], h_recv.at[q, j], partners[j][0])

    def spread_out(q):
        for j, (_, a, c) in enumerate(partners):
            await_bytes(hidden.at[q, a * 2 + c], h_recv.at[q, j])
            once(j, lambda: await_bytes(down4.at[:, a * 2 + c], d_recv.at[j]))
        units = jnp.concatenate([hidden[q, k] for k in range(4)], axis=1)
        for j, (b, peer) in enumerate(((far, to_far), (up, to_up), (dn, to_dn), (y, None))):
            sums[q, j] = dot(units, down4[b].reshape(512, LANES)).astype(BF16)
            if peer is not None:
                send(sums.at[q, j], partial_in.at[q, j], r_send.at[q], r_recv.at[q, j], peer)

    def finish(q):
        total = sums[q, 3].astype(F32)
        for j in (1, 2, 0):
            await_bytes(partial_in.at[q, j], r_recv.at[q, j])
            total = total + partial_in[q, j].astype(F32)
        row, col = iota((MAIN, 2 * PER), 0), iota((MAIN, 2 * PER), 1)
        slot = row % 16
        spread = one_hot((row // 16 == col // 2) & (slot < 14) & ((slot >= 7).astype(I32) == col % 2))
        packed = total[0:MAIN] + fold(dot(spread, total[MAIN:ROWS].astype(BF16)))
        back[pl.ds(q * PER, PER)] = packed.astype(BF16).reshape(PER, 16, LANES)
        if q == 0:
            returned[0] = back[0]

        @pl.loop(q * PER + (1 if q == 0 else 0), q * PER + PER)
        def _(place):
            send(
                back.at[place], returned.at[place], b_send, b_recv.at[q],
                (section, peer_expert(place, xh, z, 1)),
            )

    def mix(q):
        skip = 1 if q == 0 else 0
        await_bytes(returned.at[pl.ds(q * PER + skip, PER - skip)], b_recv.at[q])
        got = returned[pl.ds(q * PER, PER)].reshape(MAIN, LANES)
        picked = dot(picks[q, 0], got) + dot(picks[q, 1], unfold(got))
        total0[...] += picked[0:TOK]
        total1[...] += picked[TOK : 2 * TOK]

    tasks = {
        "S": dispatch_far, "W": prepare_weights, "K": prepare_mix,
        "U": unpack, "X": relay, "Y0": relay_up, "Y1": relay_dn,
        "C1": contract, "C2": activate, "R1": spread_out, "R4": finish, "Z": mix,
        "D": lambda i: give_down(2 - i % 2, i // 2),
    }
    for name, q in ORDER:
        tasks[name](q)

    weights = [column_of(gate_weight[k : k + 1, :]) for k in range(2)]
    mixed = weights[0] * total0[...] + weights[1] * total1[...]
    out[...] = mixed[:, 0:FEAT].astype(BF16)

    await_bytes(pack.at[pl.ds(1, 31)], z_send)
    await_bytes(back.at[pl.ds(1, 31)], b_send)
    await_bytes(wide_peer, v_send)
    await_bytes(down.at[pl.ds(0, 12)], d_send)
    for q in range(GROUPS):
        await_bytes(blocks.at[q, pl.ds(0, 7)], g_send.at[q])
        await_bytes(half_out.at[q], p_send.at[q])
        await_bytes(hidden.at[q, pl.ds(0, 3)], h_send.at[q])
        await_bytes(sums.at[q, pl.ds(0, 3)], r_send.at[q])


def on_device(tokens, norm_gain, expert_ids, gate_weight, w_gate, w_up, w_down):
    dma = pltpu.SemaphoreType.DMA
    block = (ROWS, LANES)
    return pl.pallas_call(
        kernel,
        out_shape=jax.ShapeDtypeStruct((TOK, FEAT), BF16),
        in_specs=[pl.BlockSpec(memory_space=pl.ANY)] * 7,
        out_specs=pl.BlockSpec(memory_space=pltpu.VMEM),
        scratch_shapes=[
            pltpu.VMEM((TOK, FEAT), BF16),
            pltpu.VMEM((2, TOK), I32),
            pltpu.VMEM((2, TOK), F32),
            pltpu.VMEM((1, FEAT), BF16),
            pltpu.VMEM((32, 16, LANES), BF16),
            pltpu.VMEM((32, 16, LANES), BF16),
            pltpu.VMEM((GROUPS, 8) + block, BF16),
            pltpu.VMEM((16, LANES, LANES), BF16),
            pltpu.VMEM((8, LANES, LANES), BF16),
            pltpu.VMEM((16, 128, LANES), BF16),
            pltpu.VMEM((128, D), BF16),
            pltpu.VMEM((4, 4, 128, LANES), BF16),
            pltpu.VMEM((GROUPS, ROWS, LANES + 128), F32),
            pltpu.VMEM((GROUPS, ROWS, LANES + 128), F32),
            pltpu.VMEM((GROUPS, ROWS, LANES + 128), F32),
            pltpu.VMEM((GROUPS, 4, ROWS, 128), BF16),
            pltpu.VMEM((GROUPS, 4) + block, BF16),
            pltpu.VMEM((GROUPS, 3) + block, BF16),
            pltpu.VMEM((32, 16, LANES), BF16),
            pltpu.VMEM((32, 16, LANES), BF16),
            pltpu.VMEM((GROUPS, 2, 2 * TOK, MAIN), BF16),
            pltpu.VMEM((TOK, LANES), F32),
            pltpu.VMEM((TOK, LANES), F32),
            dma((4,)), dma((5,)), dma, dma, dma, dma((3,)), dma, dma((GROUPS,)),
            dma((GROUPS,)), dma((GROUPS,)), dma((GROUPS, 6)), dma((GROUPS,)), dma((GROUPS,)),
            dma((GROUPS,)), dma((GROUPS, 3)), dma((GROUPS,)), dma((GROUPS, 3)), dma, dma((GROUPS,)),
            pltpu.SemaphoreType.REGULAR,
        ],
        compiler_params=pltpu.CompilerParams(
            collective_id=0, has_side_effects=True, vmem_limit_bytes=60 * 1024 * 1024
        ),
        cost_estimate=pl.CostEstimate(flops=2_000_000_000, bytes_accessed=3_000_000, transcendentals=73728),
    )(
        tokens, expert_ids.T, gate_weight.T, norm_gain,
        w_gate.reshape(8, 2, FEAT, 128), w_up.reshape(8, 2, FEAT, 128), w_down[0],
    )


def solution(mesh):
    placed = (
        P("expert", "section"),
        P(None, "section"),
        P("expert", None),
        P("expert", None),
        P("expert", None, "section"),
        P("expert", None, "section"),
        P("expert", "section", None),
    )
    return jax.shard_map(
        on_device, mesh=mesh, in_specs=placed, out_specs=P("expert", "section"), check_vma=False
    )
```

```python
import jax
import jax.numpy as jnp
from jax import lax
from jax.experimental import pallas as pl
from jax.experimental.pallas import tpu as pltpu
from jax.sharding import PartitionSpec as P

epsilon = 1e-06
D = 3584
FEAT = 224
LANES = 256
TOK = 144
SLOTS = 16
GROUPS = 4
PER = 8
MAIN = PER * SLOTS
ROWS = MAIN + 2 * PER
F32 = jnp.float32
BF16 = jnp.bfloat16
I32 = jnp.int32
MESH = pl.DeviceIdType.MESH
NEAR_ORDER = (0, 1)
FAR_ORDER = (3, 2)
MODES = "xxXX"
ORDER = (
    ("W", 0), ("K", 0), ("S", 3), ("U", 0), ("U", 1), ("D", 3), ("X", 0), ("Y0", 0), ("D", 5), ("X", 1),
    ("S", 2), ("D", 4), ("Y1", 0), ("Y1", 1), ("D", 0), ("Y0", 1), ("U", 3), ("D", 7), ("D", 1), ("D", 2),
    ("X", 3), ("C1", 1), ("U", 2), ("C2", 1), ("C1", 0), ("X", 2), ("D", 6), ("C2", 0), ("C1", 3), ("C2", 3),
    ("R1", 1), ("C1", 2), ("R1", 3), ("C2", 2), ("R4", 1), ("R1", 2), ("R4", 3), ("Z", 1), ("R1", 0), ("R4", 2),
    ("R4", 0), ("Z", 3), ("Z", 0), ("Z", 2),
)


def iota(shape, dim):
    return lax.broadcasted_iota(I32, shape, dim)


def one_hot(mask):
    return jnp.where(mask, 1.0, 0.0).astype(BF16)


def dot(a, b):
    return jnp.dot(a, b, preferred_element_type=F32)


def peer_expert(place, xh, z, sign):
    step = place // 2
    half = (step + 1) // 2
    offset = half * (2 * (step % 2) - 1) * (1 - 2 * (place % 2))
    return ((xh + place % 2) % 2) * 16 + (z + sign * offset + 16) % 16


def piece_of(slot):
    return slot - 7 * (slot >= 7).astype(I32)


def unfold(packed):
    rows = packed.shape[0]
    lane = iota((128, LANES), 1)
    spread = one_hot((iota((128, LANES), 0) - 96 == lane % 32) & (lane < FEAT))
    copies = dot(packed[:, 128:256], spread)
    slot = iota((rows, LANES), 0) % 16
    keep = (iota((rows, LANES), 1) // 32 == piece_of(slot)) & (slot < 14)
    return jnp.where(keep, copies, 0.0).astype(BF16)


def fold(spread):
    rows, width = spread.shape
    slot = iota((rows, width), 0) % 16
    keep = (iota((rows, width), 1) // 32 == piece_of(slot)) & (slot < 14)
    own = jnp.where(keep, spread, 0.0).astype(BF16)
    lane = iota((width, LANES), 1)
    gather = one_hot((lane >= FEAT) & (iota((width, LANES), 0) % 32 == lane - FEAT))
    return dot(own, gather)


def kernel(
    tokens_hbm, ids_hbm, gate_hbm, gain_hbm, w_gate, w_up, w_down, out,
    tokens, ids, gate_weight, gain,
    pack, arrived, blocks, wide, wide_peer, down, down_raw, down4, half_own, half_out, half_in, hidden,
    sums, partial_in, back, returned, picks, total0, total1,
    in_sem, w_sem, v_send, v_recv, d_send, d_recv, z_send, z_recv, g_send, g_x, g_y, p_send, p_recv,
    h_send, h_recv, r_send, r_recv, b_send, b_recv, near_sem,
):
    section, expert = lax.axis_index("section"), lax.axis_index("expert")
    xl, y, core = section // 8, (section // 2) % 4, section % 2
    xh, z = expert // 16, expert % 16
    up, dn, far = (y + 1) % 4, (y + 3) % 4, (y + 2) % 4
    ox = 1 - xl
    corner = xl * 2 + core

    def sec(a, b, c):
        return ((a * 4 + b) * 2 + c, expert)

    to_x, to_up, to_dn, to_core = sec(ox, y, core), sec(xl, up, core), sec(xl, dn, core), sec(xl, y, 1 - core)
    to_far, to_diagonal = sec(xl, far, core), sec(ox, y, 1 - core)
    partners = ((to_core, xl, 1 - core), (to_x, ox, core), (to_diagonal, ox, 1 - core))

    inputs = []
    for j, (src, dst) in enumerate(((ids_hbm, ids), (tokens_hbm, tokens), (gain_hbm, gain), (gate_hbm, gate_weight))):
        inputs.append(pltpu.make_async_copy(src, dst, in_sem.at[j]))
    loads = []
    for half, ref in enumerate((w_gate, w_up)):
        for c in range(2):
            loads.append(
                pltpu.make_async_copy(
                    ref.at[:, c],
                    wide.at[pl.ds(8 * c, 8), pl.ds(0, FEAT), pl.ds(128 * half, 128)],
                    w_sem.at[2 * half + c],
                )
            )
    loads.append(pltpu.make_async_copy(w_down, down_raw, w_sem.at[4]))
    for load in inputs + loads:
        load.start()

    barrier = pltpu.get_barrier_semaphore()
    for peer in (to_core, to_x, to_diagonal, to_up, to_dn, to_far):
        pl.semaphore_signal(barrier, inc=1, device_id=peer, device_id_type=MESH)

    @pl.loop(1, 18)
    def _(place):
        pl.semaphore_signal(
            barrier, inc=1, device_id=(section, peer_expert(place, xh, z, 1)), device_id_type=MESH
        )

    def send(src, dst, send_sem, recv_sem, peer):
        pltpu.make_async_remote_copy(
            src_ref=src, dst_ref=dst, send_sem=send_sem, recv_sem=recv_sem, device_id=peer, device_id_type=MESH
        ).start()

    def await_bytes(ref, sem):
        pltpu.make_async_copy(ref, ref, sem).wait()

    for load in inputs:
        load.wait()
    keys = []
    named = [(iota((32, TOK), 0) == ids[k : k + 1, :]) for k in range(2)]
    before = dot(
        one_hot(named[0] | named[1]), one_hot(iota((TOK, TOK), 0) < iota((TOK, TOK), 1))
    )
    for k in range(2):
        number = jnp.sum(jnp.where(named[k], before, 0.0), axis=0, keepdims=True)
        keys.append(ids[k : k + 1, :] * 32 + number.astype(I32))
    row = iota((512, 1), 0)
    base, slot = peer_expert(row // 16, xh, z, -1) * 32, row % 16
    main_key = base + slot
    rest_key = jnp.where(slot < 14, base + 16 + (slot >= 7).astype(I32), -1)
    to_main = one_hot((keys[0] == main_key) | (keys[1] == main_key))
    to_rest = one_hot((keys[0] == rest_key) | (keys[1] == rest_key))
    widen = one_hot(iota((FEAT, LANES), 0) == iota((FEAT, LANES), 1))
    padded = dot(tokens[...], widen).astype(BF16)
    packed = dot(to_main, padded) + fold(dot(to_rest, padded))
    pack[...] = packed.astype(BF16).reshape(32, 16, LANES)
    arrived[0] = pack[0]
    gain_row = dot(jnp.broadcast_to(gain[...], (16, FEAT)), widen)[0:1, :]

    pl.semaphore_wait(barrier, 23)
    for step in (4, 12):
        quarter = (section, xh * 16 + (z + step) % 16)
        pl.semaphore_signal(near_sem, inc=1, device_id=quarter, device_id_type=MESH)

    def dispatch(q):
        @pl.loop(q * PER + (1 if q == 0 else 0), q * PER + PER)
        def _(place):
            send(
                pack.at[place], arrived.at[place], z_send, z_recv.at[q],
                (section, peer_expert(place, xh, z, -1)),
            )

    def dispatch_far(q):
        if q == FAR_ORDER[0]:
            pl.semaphore_wait(near_sem, 2)
        dispatch(q)

    for q in NEAR_ORDER:
        dispatch(q)

    def column_of(line):
        same = iota((TOK, TOK), 0) == iota((TOK, TOK), 1)
        return jnp.sum(jnp.where(same, line, jnp.zeros_like(line)), axis=1, keepdims=True)

    def prepare_mix(_):
        for k in range(2):
            key = column_of(keys[k].astype(F32)).astype(I32)
            for q in range(GROUPS):
                column = iota((1, MAIN), 1) + q * MAIN
                base, slot = peer_expert(column // 16, xh, z, -1) * 32, column % 16
                rest_key = jnp.where(slot < 14, base + 16 + (slot >= 7).astype(I32), -1)
                picks[q, 0, pl.ds(k * TOK, TOK), :] = one_hot(key == base + slot)
                picks[q, 1, pl.ds(k * TOK, TOK), :] = one_hot(key == rest_key)
        total0[...] = jnp.zeros_like(total0)
        total1[...] = jnp.zeros_like(total1)

    def prepare_weights(_):
        wide[:, FEAT:LANES, :] = jnp.zeros((16, LANES - FEAT, LANES), BF16)
        for load in loads:
            load.wait()
        send(wide.at[pl.ds((1 - core) * 8, 8)], wide_peer, v_send, v_recv, to_core)
        for s in range(16):
            first = (s * FEAT) // 128 * 128
            shift = s * FEAT - first
            window = down_raw[:, first : min(first + 384, D)]
            place = (s % 2) * 8 + s // 2
            down[place, :, 0:FEAT] = window.astype(F32)[:, shift : shift + FEAT].astype(BF16)
            down[place, :, FEAT:LANES] = jnp.zeros((128, LANES - FEAT), BF16)
        for b in range(4):
            down4[b, corner] = down[core * 8 + chip(xl, b)]
            give_down(0, b)

    def give_down(j, b):
        peer, a, c = partners[j]
        send(down.at[c * 8 + chip(a, b)], down4.at[b, corner], d_send, d_recv.at[j], peer)

    def chip(a, b):
        return a * 4 + b

    def share(q, a, b, peer, recv_sem):
        ref = blocks.at[q, chip(a, b)]
        send(ref, ref, g_send.at[q], recv_sem, peer)

    def await_block(q, a, b, sem):
        await_bytes(blocks.at[q, chip(a, b)], sem)

    def unpack(q):
        skip = 1 if q == 0 else 0
        await_bytes(arrived.at[pl.ds(q * PER + skip, PER - skip)], z_recv.at[q])
        got = arrived[pl.ds(q * PER, PER)].reshape(MAIN, LANES)
        lane = iota((ROWS, LANES), 1)
        row, col = iota((2 * PER, MAIN), 0), iota((2 * PER, MAIN), 1)
        slot = col % 16
        gather = one_hot((col // 16 == row // 2) & (slot < 14) & ((slot >= 7).astype(I32) == row % 2))
        rest = dot(gather, unfold(got))
        x = jnp.where(lane < FEAT, jnp.concatenate([got.astype(F32), rest], axis=0), 0.0)
        square = jnp.sum(x * x, axis=1, keepdims=True)
        high = square.astype(BF16).astype(F32)
        mid = (square - high).astype(BF16).astype(F32)
        low = square - high - mid
        x = x * gain_row
        x = jnp.where(lane == FEAT, high, x)
        x = jnp.where(lane == FEAT + 1, mid, x)
        x = jnp.where(lane == FEAT + 2, low, x)
        blocks[q, chip(xl, y)] = x.astype(BF16)
        share(q, xl, y, to_x, g_x.at[q])
        share(q, xl, y, to_up, g_y.at[q, 0])
        share(q, xl, y, to_dn, g_y.at[q, 1])
        if MODES[q] != "x":
            share(q, xl, y, to_far, g_y.at[q, 4])

    def relay_to_y(q):
        await_block(q, ox, y, g_x.at[q])
        share(q, ox, y, to_up, g_y.at[q, 2])
        share(q, ox, y, to_dn, g_y.at[q, 3])
        if MODES[q] != "x":
            share(q, ox, y, to_far, g_y.at[q, 5])

    def relay_to_x(q):
        for j, (b, onward) in enumerate(((dn, 2), (up, 3), (far, 5))):
            await_block(q, xl, b, g_y.at[q, (0, 1, 4)[j]])
            share(q, xl, b, to_x, g_y.at[q, onward])

    def await_column(q):
        for b, sem in ((dn, 0), (up, 1), (far, 4)):
            await_block(q, xl, b, g_y.at[q, sem])

    def by_core(first, second):
        pl.when(core == 0)(first)
        pl.when(core == 1)(second)

    def relay(q):
        if MODES[q] == "M":
            by_core(lambda: relay_to_y(q), lambda: relay_to_x(q))
        else:
            relay_to_y(q)

    def relay_up(q):
        await_block(q, xl, dn, g_y.at[q, 0])
        share(q, xl, dn, to_up, g_y.at[q, 4])

    def relay_dn(q):
        await_block(q, ox, up, g_y.at[q, 3])
        share(q, ox, up, to_dn, g_y.at[q, 5])

    waited = set()

    def once(name, wait):
        if name not in waited:
            waited.add(name)
            wait()

    def contract(q):
        if MODES[q] == "x":
            await_block(q, xl, up, g_y.at[q, 1])
            await_block(q, ox, dn, g_y.at[q, 2])
            await_block(q, xl, far, g_y.at[q, 4])
        else:
            if MODES[q] == "X":
                await_column(q)
            else:
                by_core(lambda: await_column(q), lambda: await_block(q, ox, y, g_x.at[q]))
            await_block(q, ox, dn, g_y.at[q, 2])
            await_block(q, ox, up, g_y.at[q, 3])
        await_block(q, ox, far, g_y.at[q, 5])
        once("wide", lambda: await_bytes(wide_peer, v_recv))
        own = jnp.zeros((ROWS, LANES), F32)
        other = jnp.zeros((ROWS, LANES), F32)
        squares = jnp.zeros((ROWS, 128), F32)
        for k in range(8):
            x = blocks[q, k]
            own = own + dot(x, wide[core * 8 + k])
            other = other + dot(x, wide_peer[k])
            squares = squares + x[:, 128:256].astype(F32)
        half_out[q, :, 0:LANES] = other
        half_out[q, :, LANES : LANES + 128] = squares
        send(half_out.at[q], half_in.at[q], p_send.at[q], p_recv.at[q], to_core)
        half_own[q, :, 0:LANES] = own
        half_own[q, :, LANES : LANES + 128] = squares

    def activate(q):
        await_bytes(half_in.at[q], p_recv.at[q])
        both = half_own[q] + half_in[q]
        lane = iota((ROWS, 128), 1)
        kept = (lane >= FEAT - 128) & (lane < FEAT - 128 + 3)
        square = jnp.sum(jnp.where(kept, both[:, LANES : LANES + 128], 0.0), axis=1, keepdims=True)
        scale = lax.rsqrt(square * (1.0 / D) + epsilon)
        gate, upward = both[:, 0:128] * scale, both[:, 128:256] * scale
        hidden[q, corner] = (gate / (1.0 + jnp.exp(-gate)) * upward).astype(BF16)
        for j in (2, 1, 0):
            send(hidden.at[q, corner], hidden.at[q, corner], h_send.at[q], h_recv.at[q, j], partners[j][0])

    def spread_out(q):
        for j, (_, a, c) in enumerate(partners):
            await_bytes(hidden.at[q, a * 2 + c], h_recv.at[q, j])
            once(j, lambda: await_bytes(down4.at[:, a * 2 + c], d_recv.at[j]))
        units = jnp.concatenate([hidden[q, k] for k in range(4)], axis=1)
        for j, (b, peer) in enumerate(((far, to_far), (up, to_up), (dn, to_dn), (y, None))):
            sums[q, j] = dot(units, down4[b].reshape(512, LANES)).astype(BF16)
            if peer is not None:
                send(sums.at[q, j], partial_in.at[q, j], r_send.at[q], r_recv.at[q, j], peer)

    def finish(q):
        total = sums[q, 3].astype(F32)
        for j in (1, 2, 0):
            await_bytes(partial_in.at[q, j], r_recv.at[q, j])
            total = total + partial_in[q, j].astype(F32)
        row, col = iota((MAIN, 2 * PER), 0), iota((MAIN, 2 * PER), 1)
        slot = row % 16
        spread = one_hot((row // 16 == col // 2) & (slot < 14) & ((slot >= 7).astype(I32) == col % 2))
        packed = total[0:MAIN] + fold(dot(spread, total[MAIN:ROWS].astype(BF16)))
        back[pl.ds(q * PER, PER)] = packed.astype(BF16).reshape(PER, 16, LANES)
        if q == 0:
            returned[0] = back[0]

        @pl.loop(q * PER + (1 if q == 0 else 0), q * PER + PER)
        def _(place):
            send(
                back.at[place], returned.at[place], b_send, b_recv.at[q],
                (section, peer_expert(place, xh, z, 1)),
            )

    def mix(q):
        skip = 1 if q == 0 else 0
        await_bytes(returned.at[pl.ds(q * PER + skip, PER - skip)], b_recv.at[q])
        got = returned[pl.ds(q * PER, PER)].reshape(MAIN, LANES)
        picked = dot(picks[q, 0], got) + dot(picks[q, 1], unfold(got))
        total0[...] += picked[0:TOK]
        total1[...] += picked[TOK : 2 * TOK]

    tasks = {
        "S": dispatch_far, "W": prepare_weights, "K": prepare_mix,
        "U": unpack, "X": relay, "Y0": relay_up, "Y1": relay_dn,
        "C1": contract, "C2": activate, "R1": spread_out, "R4": finish, "Z": mix,
        "D": lambda i: give_down(2 - i % 2, i // 2),
    }
    for name, q in ORDER:
        tasks[name](q)

    weights = [column_of(gate_weight[k : k + 1, :]) for k in range(2)]
    mixed = weights[0] * total0[...] + weights[1] * total1[...]
    out[...] = mixed

    await_bytes(pack.at[pl.ds(1, 31)], z_send)
    await_bytes(back.at[pl.ds(1, 31)], b_send)
    await_bytes(wide_peer, v_send)
    await_bytes(down.at[pl.ds(0, 12)], d_send)
    for q in range(GROUPS):
        await_bytes(blocks.at[q, pl.ds(0, 7)], g_send.at[q])
        await_bytes(half_out.at[q], p_send.at[q])
        await_bytes(hidden.at[q, pl.ds(0, 3)], h_send.at[q])
        await_bytes(sums.at[q, pl.ds(0, 3)], r_send.at[q])


def on_device(tokens, norm_gain, expert_ids, gate_weight, w_gate, w_up, w_down):
    dma = pltpu.SemaphoreType.DMA
    block = (ROWS, LANES)
    mixed = pl.pallas_call(
        kernel,
        out_shape=jax.ShapeDtypeStruct((TOK, LANES), F32),
        in_specs=[pl.BlockSpec(memory_space=pl.ANY)] * 7,
        out_specs=pl.BlockSpec(memory_space=pltpu.VMEM),
        scratch_shapes=[
            pltpu.VMEM((TOK, FEAT), BF16),
            pltpu.VMEM((2, TOK), I32),
            pltpu.VMEM((2, TOK), F32),
            pltpu.VMEM((1, FEAT), BF16),
            pltpu.VMEM((32, 16, LANES), BF16),
            pltpu.VMEM((32, 16, LANES), BF16),
            pltpu.VMEM((GROUPS, 8) + block, BF16),
            pltpu.VMEM((16, LANES, LANES), BF16),
            pltpu.VMEM((8, LANES, LANES), BF16),
            pltpu.VMEM((16, 128, LANES), BF16),
            pltpu.VMEM((128, D), BF16),
            pltpu.VMEM((4, 4, 128, LANES), BF16),
            pltpu.VMEM((GROUPS, ROWS, LANES + 128), F32),
            pltpu.VMEM((GROUPS, ROWS, LANES + 128), F32),
            pltpu.VMEM((GROUPS, ROWS, LANES + 128), F32),
            pltpu.VMEM((GROUPS, 4, ROWS, 128), BF16),
            pltpu.VMEM((GROUPS, 4) + block, BF16),
            pltpu.VMEM((GROUPS, 3) + block, BF16),
            pltpu.VMEM((32, 16, LANES), BF16),
            pltpu.VMEM((32, 16, LANES), BF16),
            pltpu.VMEM((GROUPS, 2, 2 * TOK, MAIN), BF16),
            pltpu.VMEM((TOK, LANES), F32),
            pltpu.VMEM((TOK, LANES), F32),
            dma((4,)), dma((5,)), dma, dma, dma, dma((3,)), dma, dma((GROUPS,)),
            dma((GROUPS,)), dma((GROUPS,)), dma((GROUPS, 6)), dma((GROUPS,)), dma((GROUPS,)),
            dma((GROUPS,)), dma((GROUPS, 3)), dma((GROUPS,)), dma((GROUPS, 3)), dma, dma((GROUPS,)),
            pltpu.SemaphoreType.REGULAR,
        ],
        compiler_params=pltpu.CompilerParams(
            collective_id=0, has_side_effects=True, vmem_limit_bytes=60 * 1024 * 1024
        ),
        cost_estimate=pl.CostEstimate(flops=2_000_000_000, bytes_accessed=3_000_000, transcendentals=73728),
    )(
        tokens, expert_ids.T, gate_weight.T, norm_gain,
        w_gate.reshape(8, 2, FEAT, 128), w_up.reshape(8, 2, FEAT, 128), w_down[0],
    )
    return mixed[:, 0:FEAT].astype(BF16)


def solution(mesh):
    placed = (
        P("expert", "section"),
        P(None, "section"),
        P("expert", None),
        P("expert", None),
        P("expert", None, "section"),
        P("expert", None, "section"),
        P("expert", "section", None),
    )
    return jax.shard_map(
        on_device, mesh=mesh, in_specs=placed, out_specs=P("expert", "section"), check_vma=False
    )
```
